256 devices in a mesh: row: 8 (over x_hi, y), col: 32 (over z, x_lo, core).
Axes of the slice: x: 4 (x_hi: 2, x_lo: 2; x = x_hi * 2 + x_lo), y: 4, z: 8, core: 2. Of those that a mesh axis runs over, the one named last changes fastest.
Arguments:
- pointmaps: bfloat16 [64, 64, 2, 3, 14336], P('row', 'col'), may hold values from -6 to 6
- confidence: bfloat16 [64, 64, 2, 14336], P('row', 'col'), may hold values from 1 to 10
- valid_blocks: int32 [64, 64, 64], P('row', 'col'), may hold values 0 or 1
- log_depth: float32 [64, 14336], P('row', 'col'), may hold values from 0 to 1.4
- camera: float32 [64, 8], replicated, may hold values from -1 to 5.8, as said below
- pair_pose: float32 [64, 64, 8], P('row', 'col'), may hold values from -1 to 1.2, as said below
- step_sizes: float32 [3], replicated, may hold values from 0.02 to 0.2
Outputs:
- new_log_depth: float32 [64, 14336], P('row', 'col')
- new_camera: float32 [64, 8], replicated
- new_pair_pose: float32 [64, 64, 8], P('row', 'col')
The draws below stay inside these ranges and needn't reach their ends.
Inputs may be any that keep to these rules, and one draw needn't show every extreme that they name: `camera`: columns 0 to 3 hold a quaternion whose first entry lies in 0.8 to 1.2 and the others in -0.3 to 0.3; columns 4 to 6 a translation in -1 to 1; column 7 a log focal length in pixels, 5.2 to 5.8. `pair_pose`: columns 0 to 3 hold a quaternion whose first entry lies in 0.8 to 1.2 and the others in -0.3 to 0.3; columns 4 to 6 a translation in -1 to 1; column 7 a log scale in -0.5 to 0.5.
All inputs are finite; a program needn't handle non-finite values. No bound on the sum of `valid_blocks` on one device may be relied on, other than what follows from the above.
Results may differ from the reference program's by a relative error of at most 0.00055.
Values sent between devices are 32-bit elements; how exact they have to be, the bound alone decides.
A program may use at most 64 MiB of HBM per device.

```python
import math
import jax
import jax.numpy as jnp
from jax import lax

IMAGES = 64
IMG_WIDTH = 224
IMG_HEIGHT = 224
WIN_ROWS = 64
ADAM_STEPS = 2
PIXELS = 14336


def draw_camera(key, part):
    key = jax.random.fold_in(key, 11)
    keys = jax.random.split(key, 4)
    leading = jax.random.uniform(keys[0], (IMAGES, 1), jnp.float32, 0.8, 1.2)
    others = jax.random.uniform(keys[1], (IMAGES, 3), jnp.float32, -0.3, 0.3)
    shift = jax.random.uniform(keys[2], (IMAGES, 3), jnp.float32, -1.0, 1.0)
    focal_log = jax.random.uniform(keys[3], (IMAGES, 1), jnp.float32, 5.2, 5.8)
    return jnp.concatenate([leading, others, shift, focal_log], axis=1)


def draw_pair_pose(key, part):
    key = jax.random.fold_in(key, 23)
    keys = jax.random.split(key, 4)
    leading = jax.random.uniform(keys[0], (IMAGES, IMAGES, 1), jnp.float32, 0.8, 1.2)
    others = jax.random.uniform(keys[1], (IMAGES, IMAGES, 3), jnp.float32, -0.3, 0.3)
    shift = jax.random.uniform(keys[2], (IMAGES, IMAGES, 3), jnp.float32, -1.0, 1.0)
    scale_log = jax.random.uniform(keys[3], (IMAGES, IMAGES, 1), jnp.float32, -0.5, 0.5)
    return jnp.concatenate([leading, others, shift, scale_log], axis=2)


def touch_ends(drawn, rng, smallest, largest):
    longest = drawn.shape.index(max(drawn.shape))
    spots = []
    for shift in (0, 1):
        where = [jax.random.randint(jax.random.fold_in(rng, axis), (), 0, length) for axis, length in enumerate(drawn.shape)]
        where[longest] = (where[longest] + shift) % drawn.shape[longest]
        spots.append(tuple(where))
    return drawn.at[spots[0]].set(smallest).at[spots[1]].set(largest)


def block_scale(stream_key, shape, cuts, low, top_value):
    def one(dim, shards_of):
        draws = jax.random.uniform(jax.random.fold_in(jax.random.fold_in(stream_key, 6), dim), (shards_of,), jnp.float32, low / len(cuts), top_value / len(cuts))
        return jnp.repeat(jnp.exp(draws), shape[dim] // shards_of).reshape((-1,) + (1,) * (len(shape) - dim - 1))

    gain = one(*cuts[0])
    for cut in cuts[1:]:
        gain = gain * one(*cut)
    return gain


def bell_draw(own_key, dims, spread, bound, shards=(), held_as=jnp.bfloat16):
    entries = spread * jax.random.normal(own_key, dims, jnp.float32)
    if shards:
        entries = entries * block_scale(own_key, dims, shards, -0.22, 0.18)
    return jnp.clip(entries, -bound, bound).astype(held_as)


def setup_inputs(seed: int = 0) -> dict:
    key_of = jax.random.split(jax.random.key(seed), 8)
    pointmaps = bell_draw(key_of[0], (IMAGES, IMAGES, 2, 3, PIXELS), 1.0, 6.0, ((0, 8), (1, 32)))
    confidence = jnp.clip(jnp.exp(math.log(10.0) - 2.3025851 * jax.random.uniform(key_of[1], (IMAGES, IMAGES, 2, PIXELS), jnp.float32) ** block_scale(key_of[1], (IMAGES, IMAGES, 2, PIXELS), ((0, 8), (1, 32)), -0.2, 0.2)), 1.0, 10.0).astype(jnp.bfloat16)
    valid_blocks = touch_ends((jax.random.randint(key_of[2], (IMAGES, IMAGES, WIN_ROWS), 0, 4) < 3).astype(jnp.int32), jax.random.fold_in(key_of[2], 1), 0, 1)
    log_depth = jnp.clip(1.4 * jax.random.uniform(key_of[3], (IMAGES, PIXELS), jnp.float32) ** block_scale(key_of[3], (IMAGES, PIXELS), ((0, 8), (1, 32)), -0.2, 0.2), 0.0, 1.4)
    camera = draw_camera(jax.random.fold_in(key_of[7], 71), 0)
    pair_pose = draw_pair_pose(jax.random.fold_in(key_of[7], 71), 0)
    step_sizes = jnp.clip(jax.random.uniform(key_of[6], (3,), jnp.float32, 0.02, 0.2), 0.02, 0.2)
    return dict(pointmaps=pointmaps, confidence=confidence, valid_blocks=valid_blocks, log_depth=log_depth, camera=camera, pair_pose=pair_pose, step_sizes=step_sizes)


BETA_ONE = 0.9
BETA_TWO = 0.999
ADAM_EPS = 0.001
SOFTEN = 0.01

def rotation(quaternion):
    length = jnp.sqrt(lax.optimization_barrier(jnp.sum(quaternion * quaternion, axis=-1)))
    w = quaternion[..., 0] / length
    x = quaternion[..., 1] / length
    y = quaternion[..., 2] / length
    z = quaternion[..., 3] / length
    return [[1.0 - 2.0 * (y * y + z * z), 2.0 * (x * y - w * z), 2.0 * (x * z + w * y)], [2.0 * (x * y + w * z), 1.0 - 2.0 * (x * x + z * z), 2.0 * (y * z - w * x)], [2.0 * (x * z - w * y), 2.0 * (y * z + w * x), 1.0 - 2.0 * (x * x + y * y)]]

def world_points(log_depths, cameras):
    pixel_count = log_depths.shape[-1]
    position = jnp.arange(pixel_count, dtype=jnp.int32)
    across = (position % IMG_WIDTH).astype(jnp.float32) - (IMG_WIDTH - 1) / 2.0
    downward = (position // IMG_WIDTH + (IMG_HEIGHT - WIN_ROWS) // 2).astype(jnp.float32) - (IMG_HEIGHT - 1) / 2.0
    focal_len = jnp.exp(cameras[:, 7:8])
    depth_map = jnp.exp(log_depths)
    ray_parts = (across[None, :] / focal_len * depth_map, downward[None, :] / focal_len * depth_map, depth_map)
    turned = rotation(cameras[:, 0:4])
    return [turned[k][0][:, None] * ray_parts[0] + turned[k][1][:, None] * ray_parts[1] + turned[k][2][:, None] * ray_parts[2] + cameras[:, 4 + k][:, None] for k in range(3)]

def pair_loss(first_depth, second_depth, first_camera, second_camera, pair_params, pointmaps, confidence, valid_blocks, first_ids, second_ids):
    first_world = world_points(first_depth, first_camera)
    second_world = world_points(second_depth, second_camera)
    pair_rotation = rotation(pair_params[..., 0:4])
    pair_scale = jnp.exp(pair_params[..., 7])
    pair_keep = (first_ids[:, None] != second_ids[None, :]).astype(jnp.float32)
    pixel_keep = jnp.repeat(valid_blocks.astype(jnp.float32), IMG_WIDTH, axis=2) * pair_keep[:, :, None]
    loss_sum = jnp.zeros((), jnp.float32)
    for side_index in range(2):
        if side_index == 0:
            points_side = [first_world[k][:, None, :] for k in range(3)]
        else:
            points_side = [second_world[k][None, :, :] for k in range(3)]
        source = [pointmaps[:, :, side_index, k, :].astype(jnp.float32) for k in range(3)]
        squared = SOFTEN
        for k in range(3):
            aligned = pair_scale[..., None] * (pair_rotation[k][0][..., None] * source[0] + pair_rotation[k][1][..., None] * source[1] + pair_rotation[k][2][..., None] * source[2]) + pair_params[..., 4 + k][..., None]
            residual = points_side[k] - aligned
            squared = squared + residual * residual
        weight = confidence[:, :, side_index, :].astype(jnp.float32) * pixel_keep
        loss_sum = loss_sum + jnp.sum(weight * jnp.sqrt(squared))
    return loss_sum / (2.0 * (IMAGES - 1))

def adam_step(param, grad, first, second, step_number, step_size):
    first = BETA_ONE * first + (1.0 - BETA_ONE) * grad
    second = BETA_TWO * second + (1.0 - BETA_TWO) * grad * grad
    update = step_size * (first / (1.0 - BETA_ONE ** step_number)) / (jnp.sqrt(second / (1.0 - BETA_TWO ** step_number)) + ADAM_EPS)
    return (param - update, first, second)

def reference(pointmaps, confidence, valid_blocks, log_depth, camera, pair_pose, step_sizes):
    image_ids = jnp.arange(IMAGES, dtype=jnp.int32)

    def total_loss(log_depths, cameras, pair_params):

        def one_row(image_index):
            first_depth = lax.dynamic_slice_in_dim(log_depths, image_index, 1, 0)
            first_camera = lax.dynamic_slice_in_dim(cameras, image_index, 1, 0)
            row_params = lax.dynamic_slice_in_dim(pair_params, image_index, 1, 0)
            row_points = lax.dynamic_slice_in_dim(pointmaps, image_index, 1, 0)
            row_confidence = lax.dynamic_slice_in_dim(confidence, image_index, 1, 0)
            row_valid = lax.dynamic_slice_in_dim(valid_blocks, image_index, 1, 0)
            return pair_loss(first_depth, log_depths, first_camera, cameras, row_params, row_points, row_confidence, row_valid, image_index[None], image_ids)
        return jnp.sum(lax.map(jax.checkpoint(one_row), image_ids))
    depth_now, camera_now, pair_now = (log_depth, camera, pair_pose)
    depth_first = jnp.zeros_like(log_depth)
    depth_second = jnp.zeros_like(log_depth)
    camera_first = jnp.zeros_like(camera)
    camera_second = jnp.zeros_like(camera)
    pair_first = jnp.zeros_like(pair_pose)
    pair_second = jnp.zeros_like(pair_pose)
    for step_number in range(1, ADAM_STEPS + 1):
        gradients = jax.grad(total_loss, argnums=(0, 1, 2))(depth_now, camera_now, pair_now)
        depth_now, depth_first, depth_second = adam_step(depth_now, gradients[0], depth_first, depth_second, step_number, step_sizes[0])
        camera_now, camera_first, camera_second = adam_step(camera_now, gradients[1], camera_first, camera_second, step_number, step_sizes[1])
        pair_now, pair_first, pair_second = adam_step(pair_now, gradients[2], pair_first, pair_second, step_number, step_sizes[2])
    return (depth_now, camera_now, pair_now)
```

```python
import jax
import jax.numpy as jnp
from jax import lax
from jax.experimental import pallas as pl
from jax.experimental.pallas import tpu as pltpu
from jax.sharding import PartitionSpec as P

IMAGES = 64
IMG_WIDTH = 224
IMG_HEIGHT = 224
WIN_ROWS = 64
ADAM_STEPS = 2
BETA_ONE = 0.9
BETA_TWO = 0.999
ADAM_EPS = 0.001
SOFTEN = 0.01

ROWS = 8
COLS = 32
CHIPS = COLS // 2
HALF = 448
WIDE = 512
TILES = 7
STRIP = 896
LANES = 128
MESH = pl.DeviceIdType.MESH
F32 = jnp.float32


def rotation(quaternion):
    length = jnp.sqrt(sum(value * value for value in quaternion))
    w, x, y, z = [value / length for value in quaternion]
    turned = [
        [1.0 - 2.0 * (y * y + z * z), 2.0 * (x * y - w * z), 2.0 * (x * z + w * y)],
        [2.0 * (x * y + w * z), 1.0 - 2.0 * (x * x + z * z), 2.0 * (y * z - w * x)],
        [2.0 * (x * z - w * y), 2.0 * (y * z + w * x), 1.0 - 2.0 * (x * x + y * y)],
    ]
    return turned, (w, x, y, z), length


def rotation_grad(h, unit, length):
    w, x, y, z = unit
    dw = 2.0 * (z * (h[1][0] - h[0][1]) + y * (h[0][2] - h[2][0]) + x * (h[2][1] - h[1][2]))
    dx = 2.0 * (
        y * (h[0][1] + h[1][0]) + z * (h[0][2] + h[2][0]) + w * (h[2][1] - h[1][2]) - 2.0 * x * (h[1][1] + h[2][2])
    )
    dy = 2.0 * (
        x * (h[0][1] + h[1][0]) + z * (h[1][2] + h[2][1]) + w * (h[0][2] - h[2][0]) - 2.0 * y * (h[0][0] + h[2][2])
    )
    dz = 2.0 * (
        x * (h[0][2] + h[2][0]) + y * (h[1][2] + h[2][1]) + w * (h[1][0] - h[0][1]) - 2.0 * z * (h[0][0] + h[1][1])
    )
    along = w * dw + x * dx + y * dy + z * dz
    return [(dw - w * along) / length, (dx - x * along) / length, (dy - y * along) / length, (dz - z * along) / length]


def adam_step(param, grad, first, second, fix_one, fix_two, step_size):
    first = BETA_ONE * first + (1.0 - BETA_ONE) * grad
    second = BETA_TWO * second + (1.0 - BETA_TWO) * grad * grad
    update = step_size * (first / fix_one) / (jnp.sqrt(second / fix_two) + ADAM_EPS)
    return param - update, first, second


def lane_sum(value):
    return jnp.broadcast_to(jnp.sum(value, axis=1, keepdims=True), (8, LANES))


def full_sum(value):
    return jnp.broadcast_to(jnp.sum(jnp.sum(value, axis=0, keepdims=True), axis=1, keepdims=True), (8, LANES))


def kernel(
    maps_hbm, conf_hbm, valid_ref, depth_in, camera_in, pair_in, rates,
    depth_out, camera_out, pair_out,
    raw, raw_conf, planes, uv, coef, tmp, acc_pair, acc_row, acc_col,
    depth, depth_m, depth_v, pose, pose_m, pose_v, cam, cam_m, cam_v,
    row_depth, all_depth, col_depth,
    row_grad, row_sib, row_sum, row_recv, col_grad, col_recv, col_owner,
    cam_sib, cam_row, cam_all,
    load_sem, send_sem, recv_sem,
):
    r = lax.axis_index("row")
    c = lax.axis_index("col")
    q = lax.rem(c, 2)
    g = lax.div(c, 2)
    z = lax.div(c, 4)
    sibling = {"col": 2 * g + 1 - q}
    lane = lax.broadcasted_iota(jnp.int32, (8, LANES), 1)
    sub = lax.broadcasted_iota(jnp.int32, (8, LANES), 0)
    low = lane < 64

    def chip_at(n):
        half = lax.div(n + 1, 2)
        return lax.rem(g + 8 + half * (1 - 2 * lax.rem(n, 2)), CHIPS)

    def row_at(n):
        return lax.rem(r + 1 + n, ROWS)

    def remote(src, dst, kind, st, device):
        return pltpu.make_async_remote_copy(
            src_ref=src, dst_ref=dst, send_sem=send_sem.at[kind], recv_sem=recv_sem.at[kind, st],
            device_id=device, device_id_type=MESH,
        )

    def wait_bytes(ref, sem):
        pltpu.make_async_copy(ref, ref, sem).wait()

    def to_chips(make):
        def one(n, carry):
            make(chip_at(n)).start()
            return carry
        lax.fori_loop(0, CHIPS - 1, one, 0)

    def to_rows(make):
        def one(n, carry):
            make(row_at(n)).start()
            return carry
        lax.fori_loop(0, ROWS - 1, one, 0)

    load_maps = pltpu.make_async_copy(maps_hbm, raw, load_sem.at[0])
    load_conf = pltpu.make_async_copy(conf_hbm, raw_conf, load_sem.at[1])
    load_maps.start()
    load_conf.start()

    barrier = pltpu.get_barrier_semaphore()

    def greet_chip(n, carry):
        pl.semaphore_signal(barrier, inc=1, device_id={"col": 2 * chip_at(n) + q}, device_id_type=MESH)
        return carry

    def greet_row(n, carry):
        pl.semaphore_signal(barrier, inc=1, device_id={"row": row_at(n)}, device_id_type=MESH)
        return carry

    lax.fori_loop(0, CHIPS - 1, greet_chip, 0)
    lax.fori_loop(0, ROWS - 1, greet_row, 0)
    pl.semaphore_signal(barrier, inc=1, device_id=sibling, device_id_type=MESH)

    depth[...] = jnp.zeros_like(depth)
    depth[:, 0:HALF] = depth_in[...]
    for ref in (depth_m, depth_v, pose_m, pose_v, cam_m, cam_v):
        ref[...] = jnp.zeros_like(ref)
    for j in range(2):
        loaded = pair_in[:, j, :]
        for k in range(8):
            pose[j, k] = jnp.broadcast_to(loaded[:, k : k + 1], (8, LANES))
    cam[...] = jnp.zeros_like(cam)
    cam[:, 0:IMAGES] = camera_in[...]
    for t in range(TILES):
        position = lane + t * LANES
        downward = (
            (position >= IMG_WIDTH).astype(jnp.int32)
            + (position >= 2 * IMG_WIDTH).astype(jnp.int32)
            + (position >= 3 * IMG_WIDTH).astype(jnp.int32)
        )
        uv[t, 0] = (position - IMG_WIDTH * downward).astype(F32) - (IMG_WIDTH - 1) / 2.0
        uv[t, 1] = downward.astype(F32) + ((IMG_HEIGHT - WIN_ROWS) // 2 - (IMG_HEIGHT - 1) / 2.0)

    pl.semaphore_wait(barrier, CHIPS - 1 + ROWS - 1 + 1)

    def plane_base(j, tile, s):
        return ((j * 112 + tile) * 2 + s) * 32

    def prepare(m, carry):
        for j in range(2):
            here = valid_ref[:, j, :].astype(F32)
            lane64 = lax.broadcasted_iota(jnp.int32, (8, WIN_ROWS), 1)
            other = (ROWS * r + sub) != (2 * c + j)
            scale = jnp.where(other, 1.0 / (2.0 * (IMAGES - 1)), 0.0)
            line = [
                scale * jnp.broadcast_to(
                    jnp.sum(jnp.where(lane64 == 4 * m + a, here, 0.0), axis=1, keepdims=True), (8, LANES))
                for a in range(4)
            ]
            for t in range(TILES):
                start = pl.multiple_of(m * STRIP + t * LANES, LANES)
                tile = m * TILES + t
                base = pl.multiple_of(plane_base(j, tile, 0), 64)
                for i in range(8):
                    for k in range(3):
                        planes[pl.ds(base + 8 * k + i, 2, stride=32), :] = raw[
                            i, j, k, :, pl.ds(start, LANES)].astype(F32)
                    planes[pl.ds(base + 24 + i, 2, stride=32), :] = raw_conf[
                        i, j, :, pl.ds(start, LANES)].astype(F32)
                first = t * LANES // IMG_WIDTH
                split = (first + 1) * IMG_WIDTH - t * LANES
                keep = line[first] if split >= LANES else jnp.where(lane < split, line[first], line[first + 1])
                for s in range(2):
                    at = pl.ds(pl.multiple_of(base + 32 * s + 24, 8), 8)
                    planes[at, :] = planes[at, :] * keep
        return carry

    def camera_of_rows():
        now = cam[...]
        mine = lane == 8 * r + sub
        return [lane_sum(jnp.where(mine, jnp.broadcast_to(now[k : k + 1, :], (8, LANES)), 0.0)) for k in range(8)]

    def camera_of_col(j):
        now = cam[...]
        mine = lane == 2 * c + j
        return [full_sum(jnp.where(mine & (sub == k), now, 0.0)) for k in range(8)]

    def element(base, at, z3, total):
        x = [planes[pl.ds(pl.multiple_of(base + 8 * k, 8), 8), :] for k in range(3)]
        weight = planes[pl.ds(pl.multiple_of(base + 24, 8), 8), :]
        residual = [
            z3[k] - (at[9 + k] + at[3 * k] * x[0] + at[3 * k + 1] * x[1] + at[3 * k + 2] * x[2]) for k in range(3)
        ]
        squared = SOFTEN + residual[0] * residual[0] + residual[1] * residual[1] + residual[2] * residual[2]
        pull = weight * lax.rsqrt(squared)
        grads = [pull * residual[k] for k in range(3)]
        terms = [grads[k] * x[n] for k in range(3) for n in range(3)] + grads
        total = terms if total is None else [a + b for a, b in zip(total, terms)]
        return grads, total

    def moments(grads, value, u, v, total):
        h = [grads[k] * value for k in range(3)]
        terms = [h[k] * u for k in range(3)] + [h[k] * v for k in range(3)] + h + list(grads)
        return terms if total is None else [a + b for a, b in zip(total, terms)]

    def rays(first, t, down):
        u = uv[t, 0]
        v = uv[t, 1] + down
        return u, v, [coef[first + k] * u + (coef[first + 3 + k] * v + coef[first + 6 + k]) for k in range(3)]

    def pair_at(j, s):
        first = 27 + 15 * j
        return [coef[first + k] for k in range(9)] + [coef[first + 9 + 3 * s + k] for k in range(3)]

    def strip_tiles(left, right):
        rolled = pltpu.roll(right, 64, 1)
        middle = jnp.where(low[0 : left.shape[0]], left[:, 384:512], rolled[:, 0:128])
        return [left[:, 0:128], left[:, 128:256], left[:, 256:384], middle,
                rolled[:, 128:256], rolled[:, 256:384], rolled[:, 384:512]]

    def side_rows(st):
        def body(m, carry):
            tiles = strip_tiles(row_depth[st, 0, m], row_depth[st, 1, m])
            down = (4 * m).astype(F32)
            for t in range(TILES):
                value = jnp.exp(tiles[t])
                u, v, ray = rays(0, t, down)
                tmp[t, 6] = value
                for k in range(3):
                    tmp[t, k] = value * ray[k]
            for j in range(2):
                at = pair_at(j, 0)
                total = None
                for t in range(TILES):
                    z3 = [tmp[t, k] for k in range(3)]
                    grads, total = element(plane_base(j, m * TILES + t, 0), at, z3, total)
                    for k in range(3):
                        tmp[t, 3 + k] = grads[k] if j == 0 else tmp[t, 3 + k] + grads[k]
                for k in range(12):
                    acc_pair[j, k] += total[k]
            total = None
            out = []
            for t in range(TILES):
                grads = [tmp[t, 3 + k] for k in range(3)]
                z3 = [tmp[t, k] for k in range(3)]
                out.append(grads[0] * z3[0] + grads[1] * z3[1] + grads[2] * z3[2])
                total = moments(grads, tmp[t, 6], uv[t, 0], uv[t, 1] + down, total)
            for k in range(12):
                acc_row[k] += total[k]
            row_grad[0, m] = jnp.concatenate(out[0:4], axis=1)
            row_grad[1, m] = pltpu.roll(jnp.concatenate(out[3:7], axis=1), 448, 1)
            return carry
        return body

    def side_cols(st):
        def body(m, carry):
            tiles = strip_tiles(col_depth[st, 0, m, q], col_depth[st, 1, m, q])
            values = [jnp.exp(tile) for tile in tiles]
            down = (4 * m).astype(F32)
            for j in range(2):
                at = pair_at(j, 1)
                total = None
                cam_total = None
                out = []
                for t in range(TILES):
                    value = jnp.broadcast_to(values[t][j : j + 1, :], (8, LANES))
                    u, v, ray = rays(9 + 9 * j, t, down)
                    z3 = [value * ray[k] for k in range(3)]
                    grads, total = element(plane_base(j, m * TILES + t, 1), at, z3, total)
                    mine = grads[0] * z3[0] + grads[1] * z3[1] + grads[2] * z3[2]
                    out.append(jnp.sum(mine, axis=0, keepdims=True))
                    cam_total = moments(grads, value, u, v, cam_total)
                for k in range(12):
                    acc_pair[j, k] += total[k]
                for k in range(12):
                    acc_col[j, k] += cam_total[k]
                col_grad[st, 0, m, q, j : j + 1, :] = jnp.concatenate(out[0:4], axis=1)
                col_grad[st, 1, m, q, j : j + 1, :] = pltpu.roll(jnp.concatenate(out[3:7], axis=1), 448, 1)
            return carry
        return body

    def camera_grad(values, total):
        turned, unit, length = rotation(values[0:4])
        inverse = jnp.exp(-values[7])
        h = [[total[k] * inverse, total[3 + k] * inverse, total[6 + k]] for k in range(3)]
        focal = sum(turned[k][0] * h[k][0] + turned[k][1] * h[k][1] for k in range(3))
        return rotation_grad(h, unit, length) + [total[9], total[10], total[11], -focal]

    ROW_ALL, ROW_FWD, OWN_COL, COL_ALL, COL_FWD, GR_SIB, GR_ALL, GC_SIB, GC_ALL, GC_OWN, CA_SIB, CA_ROW, CA_ALL = range(13)

    def step(st, carry):
        late = (st > 0).astype(F32)
        fix_one = (1.0 - BETA_ONE) + late * ((1.0 - BETA_ONE**2) - (1.0 - BETA_ONE))
        fix_two = (1.0 - BETA_TWO) + late * ((1.0 - BETA_TWO**2) - (1.0 - BETA_TWO))

        now = depth[...]
        for x in range(2):
            for k in range(2):
                all_depth[st, r, x, k] = now[4 * x + 2 * k : 4 * x + 2 * k + 2, :]
        row_depth[st, q, g] = now
        to_rows(lambda p: remote(all_depth.at[st, r], all_depth.at[st, r], OWN_COL, st, {"row": p}))
        to_chips(lambda p: remote(row_depth.at[st, q, g], row_depth.at[st, q, g], ROW_ALL, st, {"col": 2 * p + q}))

        @pl.when(st == 0)
        def _():
            load_maps.wait()
            load_conf.wait()
            lax.fori_loop(0, CHIPS // 2, prepare, 0)

        @pl.when(st > 0)
        def _():
            wait_bytes(cam_all.at[st - 1, pl.ds(0, ROWS - 1)], recv_sem.at[CA_ALL, st - 1])
            grad = cam_all[st - 1, 0]
            for p in range(1, ROWS):
                grad = grad + cam_all[st - 1, p]
            cam[...], cam_m[...], cam_v[...] = adam_step(
                cam[...], grad, cam_m[...], cam_v[...], 1.0 - BETA_ONE, 1.0 - BETA_TWO, rates[1])

        wait_bytes(all_depth.at[st, pl.ds(0, ROWS - 1)], recv_sem.at[OWN_COL, st])
        col_depth[st, q, g] = all_depth[st, z, lax.rem(g, 2)]
        to_chips(lambda p: remote(
            all_depth.at[st, lax.div(p, 2), lax.rem(p, 2)], col_depth.at[st, q, g], COL_ALL, st, {"col": 2 * p + q}))

        wait_bytes(row_depth.at[st, q, pl.ds(0, CHIPS - 1)], recv_sem.at[ROW_ALL, st])
        row_fwd = remote(row_depth.at[st, q], row_depth.at[st, q], ROW_FWD, st, sibling)
        row_fwd.start()

        @pl.when(st == 0)
        def _():
            lax.fori_loop(CHIPS // 2, CHIPS, prepare, 0)

        values = camera_of_rows()
        turned, _, _ = rotation(values[0:4])
        inverse = jnp.exp(-values[7])
        shift = [[None] * 2, [None] * 2]
        for k in range(3):
            coef[k] = turned[k][0] * inverse
            coef[3 + k] = turned[k][1] * inverse
            coef[6 + k] = turned[k][2]
        shift[0][0] = shift[0][1] = values[4:7]
        for j in range(2):
            values = camera_of_col(j)
            turned, _, _ = rotation(values[0:4])
            inverse = jnp.exp(-values[7])
            for k in range(3):
                coef[9 + 9 * j + k] = turned[k][0] * inverse
                coef[9 + 9 * j + 3 + k] = turned[k][1] * inverse
                coef[9 + 9 * j + 6 + k] = turned[k][2]
            shift[1][j] = values[4:7]
        for j in range(2):
            values = [pose[j, k] for k in range(8)]
            turned, _, _ = rotation(values[0:4])
            scale = jnp.exp(values[7])
            first = 27 + 15 * j
            for k in range(3):
                for n in range(3):
                    coef[first + 3 * k + n] = scale * turned[k][n]
                for s in range(2):
                    coef[first + 9 + 3 * s + k] = values[4 + k] - shift[s][j][k]
        for ref in (acc_pair, acc_row, acc_col):
            ref[...] = jnp.zeros_like(ref)

        wait_bytes(row_depth.at[st, 1 - q], recv_sem.at[ROW_FWD, st])
        lax.fori_loop(0, CHIPS // 2, side_rows(st), 0)
        wait_bytes(col_depth.at[st, q, pl.ds(0, CHIPS - 1)], recv_sem.at[COL_ALL, st])
        col_fwd = remote(col_depth.at[st, q, :, 1 - q], col_depth.at[st, q, :, 1 - q], COL_FWD, st, sibling)
        col_fwd.start()
        lax.fori_loop(CHIPS // 2, CHIPS, side_rows(st), 0)

        row_swap = remote(row_grad.at[1 - q], row_sib.at[st], GR_SIB, st, sibling)
        row_swap.start()
        wait_bytes(col_depth.at[st, 1 - q, :, q], recv_sem.at[COL_FWD, st])
        lax.fori_loop(0, CHIPS // 2, side_cols(st), 0)
        wait_bytes(row_sib.at[st], recv_sem.at[GR_SIB, st])

        def add_sibling(m, carry):
            row_sum[m] = row_grad[q, m] + row_sib[st, m]
            return carry

        lax.fori_loop(0, CHIPS, add_sibling, 0)
        row_recv[st, g] = row_sum[g]
        to_chips(lambda p: remote(row_sum.at[p], row_recv.at[st, g], GR_ALL, st, {"col": 2 * p + q}))
        lax.fori_loop(CHIPS // 2, CHIPS, side_cols(st), 0)

        col_swap = remote(col_grad.at[st, 1 - q, :, q], col_grad.at[st, 1 - q, :, q], GC_SIB, st, sibling)
        col_swap.start()

        values = camera_of_rows()
        part = camera_grad(values, [lane_sum(acc_row[k]) for k in range(12)])
        rows = [jnp.where(lane == 8 * r + sub, part[k], 0.0) for k in range(8)]
        mine = jnp.concatenate([jnp.sum(row, axis=0, keepdims=True) for row in rows], axis=0)
        for j in range(2):
            values = camera_of_col(j)
            part = camera_grad(values, [full_sum(acc_col[j, k]) for k in range(12)])
            for k in range(8):
                mine = mine + jnp.where((sub == k) & (lane == 2 * c + j), part[k], 0.0)
        cam_sib[st, q] = mine
        cam_swap = remote(cam_sib.at[st, q], cam_sib.at[st, q], CA_SIB, st, sibling)
        cam_swap.start()

        wait_bytes(col_grad.at[st, q, :, 1 - q], recv_sem.at[GC_SIB, st])
        col_recv[st, g] = col_grad[st, q, g]
        to_chips(lambda p: remote(col_grad.at[st, q, p], col_recv.at[st, g], GC_ALL, st, {"col": 2 * p + q}))
        wait_bytes(cam_sib.at[st, 1 - q], recv_sem.at[CA_SIB, st])
        cam_row[st, g] = cam_sib[st, 0] + cam_sib[st, 1]
        to_chips(lambda p: remote(cam_row.at[st, g], cam_row.at[st, g], CA_ROW, st, {"col": 2 * p + q}))

        for j in range(2):
            values = [pose[j, k] for k in range(8)]
            total = [-lane_sum(acc_pair[j, k]) for k in range(12)]
            turned, unit, length = rotation(values[0:4])
            scale = jnp.exp(values[7])
            h = [[scale * total[3 * k + n] for n in range(3)] for k in range(3)]
            grad_scale = sum(turned[k][n] * h[k][n] for k in range(3) for n in range(3))
            grads = rotation_grad(h, unit, length) + total[9:12] + [grad_scale]
            for k in range(8):
                pose[j, k], pose_m[j, k], pose_v[j, k] = adam_step(
                    values[k], grads[k], pose_m[j, k], pose_v[j, k], fix_one, fix_two, rates[2])

        wait_bytes(row_recv.at[st, pl.ds(0, CHIPS - 1)], recv_sem.at[GR_ALL, st])
        grad = row_recv[st, 0]
        for p in range(1, CHIPS):
            grad = grad + row_recv[st, p]

        wait_bytes(cam_row.at[st, pl.ds(0, CHIPS - 1)], recv_sem.at[CA_ROW, st])
        group = cam_row[st, 0]
        for p in range(1, CHIPS):
            group = group + cam_row[st, p]
        cam_all[st, r] = group
        to_rows(lambda p: remote(cam_all.at[st, r], cam_all.at[st, r], CA_ALL, st, {"row": p}))

        wait_bytes(col_recv.at[st, pl.ds(0, CHIPS - 1)], recv_sem.at[GC_ALL, st])
        col_owner[st, r] = col_recv[st, pl.ds(2 * r, 2)]
        to_rows(lambda p: remote(col_recv.at[st, pl.ds(2 * p, 2)], col_owner.at[st, r], GC_OWN, st, {"row": p}))

        wait_bytes(all_depth.at[st, pl.ds(0, ROWS - 1)], send_sem.at[OWN_COL])
        wait_bytes(row_depth.at[st, q, pl.ds(0, CHIPS - 1)], send_sem.at[ROW_ALL])
        wait_bytes(row_depth.at[st, q], send_sem.at[ROW_FWD])
        wait_bytes(col_depth.at[st, q, pl.ds(0, CHIPS - 1)], send_sem.at[COL_ALL])
        wait_bytes(col_depth.at[st, q, :, 1 - q], send_sem.at[COL_FWD])
        wait_bytes(row_sib.at[st], send_sem.at[GR_SIB])
        wait_bytes(row_recv.at[st, pl.ds(0, CHIPS - 1)], send_sem.at[GR_ALL])
        wait_bytes(col_grad.at[st, 1 - q, :, q], send_sem.at[GC_SIB])
        wait_bytes(cam_sib.at[st, q], send_sem.at[CA_SIB])
        wait_bytes(col_recv.at[st, pl.ds(0, CHIPS - 1)], send_sem.at[GC_ALL])
        wait_bytes(cam_row.at[st, pl.ds(0, CHIPS - 1)], send_sem.at[CA_ROW])

        wait_bytes(col_owner.at[st, pl.ds(0, ROWS - 1)], recv_sem.at[GC_OWN, st])
        pieces = []
        for x in range(2):
            for k in range(2):
                piece = col_owner[st, 0, x, k]
                for p in range(1, ROWS):
                    piece = piece + col_owner[st, p, x, k]
                pieces.append(piece)
        grad = grad + jnp.concatenate(pieces, axis=0)
        depth[...], depth_m[...], depth_v[...] = adam_step(
            depth[...], grad, depth_m[...], depth_v[...], fix_one, fix_two, rates[0])

        wait_bytes(cam_all.at[st, pl.ds(0, ROWS - 1)], send_sem.at[CA_ALL])
        wait_bytes(col_owner.at[st, pl.ds(0, ROWS - 1)], send_sem.at[GC_OWN])
        return carry

    lax.fori_loop(0, ADAM_STEPS, step, 0)

    last = ADAM_STEPS - 1
    depth_out[...] = depth[:, 0:HALF]
    small = lax.broadcasted_iota(jnp.int32, (8, 8), 1)
    for j in range(2):
        packed = jnp.zeros((8, 8), F32)
        for k in range(8):
            packed = jnp.where(small == k, pose[j, k][:, 0:8], packed)
        pair_out[:, j, :] = packed
    wait_bytes(cam_all.at[last, pl.ds(0, ROWS - 1)], recv_sem.at[CA_ALL, last])
    grad = cam_all[last, 0]
    for p in range(1, ROWS):
        grad = grad + cam_all[last, p]
    final, _, _ = adam_step(
        cam[...], grad, cam_m[...], cam_v[...], 1.0 - BETA_ONE**2, 1.0 - BETA_TWO**2, rates[1])
    camera_out[...] = final[:, 0:IMAGES]


def body(pointmaps, confidence, valid_blocks, log_depth, camera, pair_pose, step_sizes):
    vmem = pl.BlockSpec(memory_space=pltpu.VMEM)
    hbm = pl.BlockSpec(memory_space=pl.ANY)
    steps = ADAM_STEPS

    def f32(*shape):
        return pltpu.VMEM(shape, F32)

    kinds = 13
    maps = pointmaps.transpose(0, 1, 3, 2, 4)
    depth, cam, pair = pl.pallas_call(
        kernel,
        out_shape=(
            jax.ShapeDtypeStruct(log_depth.shape, F32),
            jax.ShapeDtypeStruct((8, IMAGES), F32),
            jax.ShapeDtypeStruct(pair_pose.shape, F32),
        ),
        in_specs=[hbm, hbm, vmem, vmem, vmem, vmem, pl.BlockSpec(memory_space=pltpu.SMEM)],
        out_specs=(vmem, vmem, vmem),
        scratch_shapes=[
            pltpu.VMEM(maps.shape, jnp.bfloat16),
            pltpu.VMEM(confidence.shape, jnp.bfloat16),
            f32(2 * 112 * 2 * 32, LANES),
            f32(TILES, 2, 8, LANES),
            f32(57, 8, LANES),
            f32(TILES, 7, 8, LANES),
            f32(2, 12, 8, LANES),
            f32(12, 8, LANES),
            f32(2, 12, 8, LANES),
            f32(8, WIDE), f32(8, WIDE), f32(8, WIDE),
            f32(2, 8, 8, LANES), f32(2, 8, 8, LANES), f32(2, 8, 8, LANES),
            f32(8, LANES), f32(8, LANES), f32(8, LANES),
            f32(steps, 2, CHIPS, 8, WIDE),
            f32(steps, ROWS, 2, 2, 2, WIDE),
            f32(steps, 2, CHIPS, 2, 2, WIDE),
            f32(2, CHIPS, 8, WIDE),
            f32(steps, CHIPS, 8, WIDE),
            f32(CHIPS, 8, WIDE),
            f32(steps, CHIPS, 8, WIDE),
            f32(steps, 2, CHIPS, 2, 2, WIDE),
            f32(steps, CHIPS, 2, 2, WIDE),
            f32(steps, ROWS, 2, 2, 2, WIDE),
            f32(steps, 2, 8, LANES),
            f32(steps, CHIPS, 8, LANES),
            f32(steps, ROWS, 8, LANES),
            pltpu.SemaphoreType.DMA((2,)),
            pltpu.SemaphoreType.DMA((kinds,)),
            pltpu.SemaphoreType.DMA((kinds, steps)),
        ],
        compiler_params=pltpu.CompilerParams(
            collective_id=0, has_side_effects=True, vmem_limit_bytes=56 * 1024 * 1024
        ),
        name="align",
    )(maps, confidence, valid_blocks, log_depth, camera.T, pair_pose, step_sizes)
    return depth, cam.T, pair


def solution(mesh):
    in_specs = (
        P("row", "col", None, None, None),
        P("row", "col", None, None),
        P("row", "col", None),
        P("row", "col"),
        P(),
        P("row", "col", None),
        P(),
    )
    out_specs = (P("row", "col"), P(), P("row", "col", None))
    return jax.shard_map(body, mesh=mesh, in_specs=in_specs, out_specs=out_specs, check_vma=False)
```

```python
import math

import jax
import jax.numpy as jnp
import numpy as np
from jax import lax
from jax.experimental import pallas as pl
from jax.experimental.pallas import tpu as pltpu
from jax.sharding import PartitionSpec as P

IMAGES = 64
IMG_WIDTH = 224
IMG_HEIGHT = 224
WIN_ROWS = 64
ADAM_STEPS = 2
BETA_ONE = 0.9
BETA_TWO = 0.999
ADAM_EPS = 0.001
SOFTEN = 0.01

ROWS = 8
COLS = 32
CHIPS = COLS // 2
SECONDS = 4
HALF = 448
WIDE = 512
TILES = 4
STRIP = 896
LANES = 128
MESH = pl.DeviceIdType.MESH
F32 = jnp.float32


def plain_rotation(w, x, y, z):
    length = jnp.sqrt(w * w + x * x + y * y + z * z)
    w, x, y, z = w / length, x / length, y / length, z / length
    return [
        [1.0 - 2.0 * (y * y + z * z), 2.0 * (x * y - w * z), 2.0 * (x * z + w * y)],
        [2.0 * (x * y + w * z), 1.0 - 2.0 * (x * x + z * z), 2.0 * (y * z - w * x)],
        [2.0 * (x * z - w * y), 2.0 * (y * z + w * x), 1.0 - 2.0 * (x * x + y * y)],
    ]


class Pair:
    def __init__(self, high, low):
        self.high = high
        self.low = low

    @staticmethod
    def of(value):
        return value if isinstance(value, Pair) else Pair(value, None)

    @staticmethod
    def closed(high, low):
        total = high + low
        return Pair(total, low - (total - high))

    @staticmethod
    def constant(value):
        high = float(np.float32(value))
        low = value - high
        return Pair(high, low if low else None)

    def __add__(self, other):
        other = Pair.of(other)
        total = self.high + other.high
        back = total - self.high
        rest = (self.high - (total - back)) + (other.high - back)
        for part in (self.low, other.low):
            rest = rest if part is None else rest + part
        return Pair.closed(total, rest)

    def __neg__(self):
        return Pair(-self.high, None if self.low is None else -self.low)

    def __sub__(self, other):
        return self + (-Pair.of(other))

    def twice(self):
        return Pair(2.0 * self.high, None if self.low is None else 2.0 * self.low)

    @staticmethod
    def split(value):
        wide = 4097.0 * value
        top = wide - (wide - value)
        return top, value - top

    def __mul__(self, other):
        other = Pair.of(other)
        product = self.high * other.high
        a, b = Pair.split(self.high)
        c, d = Pair.split(other.high)
        rest = ((a * c - product) + a * d + b * c) + b * d
        if self.low is not None:
            rest = rest + self.low * other.high
        if other.low is not None:
            rest = rest + self.high * other.low
        return Pair.closed(product, rest)

    def __truediv__(self, other):
        other = Pair.of(other)
        first = self.high / other.high
        rest = self - other * Pair(first, None)
        return Pair.closed(first, rest.high / other.high)

    def root(self):
        first = jnp.sqrt(self.high)
        rest = self - Pair(first, None) * Pair(first, None)
        return Pair.closed(first, rest.high / (2.0 * first))


def exact_exp(value):
    small = Pair(value * 0.0625, None)
    total = Pair.constant(1.0 / math.factorial(12))
    total = Pair(jnp.full_like(value, total.high), None)
    for k in range(11, -1, -1):
        total = total * small + Pair.constant(1.0 / math.factorial(k))
    for _ in range(4):
        total = total * total
    return total


def rotation(quaternion):
    w, x, y, z = [Pair.of(value) for value in quaternion]
    length = (w * w + x * x + y * y + z * z).root()
    w, x, y, z = w / length, x / length, y / length, z / length
    xx, yy, zz = x * x, y * y, z * z
    xy, xz, yz, wx, wy, wz = x * y, x * z, y * z, w * x, w * y, w * z
    one = Pair(1.0, None)
    turned = [
        [one - (yy + zz).twice(), (xy - wz).twice(), (xz + wy).twice()],
        [(xy + wz).twice(), one - (xx + zz).twice(), (yz - wx).twice()],
        [(xz - wy).twice(), (yz + wx).twice(), one - (xx + yy).twice()],
    ]
    return turned, (w, x, y, z), length


def rotation_grad(h, unit, length):
    w, x, y, z = unit
    sums = [h[0][1] + h[1][0], h[0][2] + h[2][0], h[1][2] + h[2][1]]
    turns = [h[2][1] - h[1][2], h[0][2] - h[2][0], h[1][0] - h[0][1]]
    dw = (z * turns[2] + y * turns[1] + x * turns[0]).twice()
    dx = (y * sums[0] + z * sums[1] + w * turns[0] - (x * (h[1][1] + h[2][2])).twice()).twice()
    dy = (x * sums[0] + z * sums[2] + w * turns[1] - (y * (h[0][0] + h[2][2])).twice()).twice()
    dz = (x * sums[1] + y * sums[2] + w * turns[2] - (z * (h[0][0] + h[1][1])).twice()).twice()
    along = w * dw + x * dx + y * dy + z * dz
    return [((part - axis * along) / length).high for part, axis in ((dw, w), (dx, x), (dy, y), (dz, z))]


def adam_step(param, grad, first, second, fix_one, fix_two, step_size):
    first = BETA_ONE * first + (1.0 - BETA_ONE) * grad
    second = BETA_TWO * second + (1.0 - BETA_TWO) * grad * grad
    update = step_size * (first / fix_one) / (jnp.sqrt(second / fix_two) + ADAM_EPS)
    return param - update, first, second


def lane_sum(value):
    return jnp.broadcast_to(jnp.sum(value, axis=1, keepdims=True), value.shape)


COL_DEPTH, ROW_DEPTH, ROW_GRAD, COL_GRAD, POSE, CAM_ROW, CAM_ALL, SWAP, FIRST_POSE, OWN_DEPTH = range(10)
KINDS = 10


def kernel(
    maps_hbm, conf_hbm, valid_ref, depth_in, camera_in, pair_in, rates,
    depth_out, camera_out, pair_out,
    raw, raw_conf, planes, outbox, uv, row_ray, col_ray, turn, tmp, acc_row, acc_col, sums,
    depth, depth_m, depth_v, first_pose, pose, pose_m, pose_v, cam, cam_m, cam_v,
    row_depth, all_depth, col_depth, row_grad, row_recv, col_grad, col_recv, cam_row, cam_all,
    load_sem, send_sem, recv_sem, all_sem,
):
    r = lax.axis_index("row")
    c = lax.axis_index("col")
    q = lax.rem(c, 2)
    g = lax.div(c, 2)
    z = lax.div(g, 2)
    x_lo = lax.rem(g, 2)
    inside = r == z
    sibling = (r, 2 * g + 1 - q)
    lane = lax.broadcasted_iota(jnp.int32, (8, LANES), 1)
    sub = lax.broadcasted_iota(jnp.int32, (8, LANES), 0)

    def chip_at(n):
        half = lax.div(n + 1, 2)
        return lax.rem(g + 8 + half * (1 - 2 * lax.rem(n, 2)), CHIPS)

    def remote(src, dst, kind, st, device):
        return pltpu.make_async_remote_copy(
            src_ref=src, dst_ref=dst, send_sem=send_sem.at[kind], recv_sem=recv_sem.at[kind, st],
            device_id=device, device_id_type=MESH,
        )

    def wait_bytes(ref, sem):
        pltpu.make_async_copy(ref, ref, sem).wait()

    def wait_slots(ref, sem):
        @pl.when(inside)
        def _():
            wait_bytes(ref.at[pl.ds(0, CHIPS - 1)], sem)

        @pl.when(jnp.logical_not(inside))
        def _():
            wait_bytes(ref, sem)

    def repeat(count, action):
        def one(n, carry):
            action(n)
            return carry
        lax.fori_loop(0, count, one, 0)

    load_maps = pltpu.make_async_copy(maps_hbm, raw, load_sem.at[0])
    load_conf = pltpu.make_async_copy(conf_hbm, raw_conf, load_sem.at[1])
    load_maps.start()
    load_conf.start()

    barrier = pltpu.get_barrier_semaphore()

    def greet(row, col):
        pl.semaphore_signal(barrier, inc=1, device_id=(row, col), device_id_type=MESH)

    def to_row_group(act):
        def one(n):
            p = chip_at(n)
            act(p, r, 2 * p + q)
        repeat(CHIPS - 1, one)

    def row_near(n):
        across = lax.div(n, 4)
        turn_y = lax.rem(n, 4)
        turn_y = turn_y + lax.div(turn_y, 2) - 2 * lax.div(turn_y, 3)
        return 4 * lax.rem(lax.div(r, 4) + across, 2) + lax.rem(lax.rem(r, 4) + turn_y, 4)

    def to_column(act):
        lax.fori_loop(1, ROWS, lambda n, carry: (act(row_near(ROWS - n)), carry)[1], 0)

    def to_column_chips(act):
        def one(n):
            act(lax.rem(r + lax.div(n, 2), ROWS), 2 * g + lax.rem(q + lax.rem(n, 2), 2))
        lax.fori_loop(1, 2 * ROWS, lambda n, carry: (one(n), carry)[1], 0)

    to_row_group(lambda p, row, col: greet(row, col))
    to_column(lambda row: greet(row, c))
    greet(*sibling)

    depth[...] = jnp.zeros_like(depth)
    depth[:, 0:HALF] = depth_in[...]
    depth[...] = pltpu.roll(depth[...], 64 * q, 1)
    for ref in (depth_m, depth_v, pose_m, pose_v, cam, cam_m, cam_v):
        ref[...] = jnp.zeros_like(ref)
    for j in range(2):
        loaded = pair_in[:, j, :]
        for k in range(8):
            first_pose[q, k, 8 * j : 8 * j + 8, :] = jnp.broadcast_to(loaded[:, k : k + 1], (8, LANES))
    cam[:, 0:IMAGES] = camera_in[...]
    for t in range(TILES):
        position = lane + (3 * q + t) * LANES
        downward = (
            (position >= IMG_WIDTH).astype(jnp.int32)
            + (position >= 2 * IMG_WIDTH).astype(jnp.int32)
            + (position >= 3 * IMG_WIDTH).astype(jnp.int32)
        )
        uv[t, 0] = (position - IMG_WIDTH * downward).astype(F32) - (IMG_WIDTH - 1) / 2.0
        uv[t, 1] = downward.astype(F32) + ((IMG_HEIGHT - WIN_ROWS) // 2 - (IMG_HEIGHT - 1) / 2.0)

    def prepare(m):
        lane64 = lax.broadcasted_iota(jnp.int32, (8, WIN_ROWS), 1)
        for away in (True, False):
            half = 1 - q if away else q
            for j in range(2):
                here = valid_ref[:, j, :].astype(F32)
                other = (ROWS * r + sub) != (2 * c + j)
                scale = jnp.where(other, 1.0 / (2.0 * (IMAGES - 1)), 0.0)
                line = [
                    scale * lane_sum_to(jnp.where(lane64 == 4 * m + 2 * half + a, here, 0.0)) for a in range(2)
                ]
                for t in range(TILES):
                    tile = 3 * half + t
                    start = pl.multiple_of(m * STRIP + tile * LANES, LANES)
                    put = outbox.at[m, j, t] if away else planes.at[q, m, j, t]
                    for i in range(8):
                        for k in range(3):
                            put[pl.ds(8 * k + i, 2, stride=32), :] = raw[i, j, k, :, pl.ds(start, LANES)].astype(F32)
                        put[pl.ds(24 + i, 2, stride=32), :] = raw_conf[i, j, :, pl.ds(start, LANES)].astype(F32)
                    position = lane + tile * LANES - HALF * half
                    keep = jnp.where(position < IMG_WIDTH, line[0], line[1])
                    keep = jnp.where((position >= 0) & (position < HALF), keep, 0.0)
                    for s in range(2):
                        put[32 * s + 24 : 32 * s + 32, :] = put[32 * s + 24 : 32 * s + 32, :] * keep

    def lane_sum_to(value):
        return jnp.broadcast_to(jnp.sum(value, axis=1, keepdims=True), (8, LANES))

    def swap_strip(m):
        remote(outbox.at[m], planes.at[q, m], SWAP, 0, sibling).start()

    load_maps.wait()
    load_conf.wait()
    repeat(CHIPS // 2, prepare)
    pl.semaphore_wait(barrier, CHIPS - 1 + ROWS - 1 + 1)

    lane16 = lax.broadcasted_iota(jnp.int32, (16, LANES), 1)
    sub16 = lax.broadcasted_iota(jnp.int32, (16, LANES), 0)
    image16 = jnp.where(sub16 < 8, 8 * r + sub16, SECONDS * g + lax.rem(sub16, SECONDS))

    def cameras():
        now = cam[...]
        return [
            lane_sum(jnp.where(lane16 == image16, jnp.broadcast_to(now[k : k + 1, :], (16, LANES)), 0.0))
            for k in range(8)
        ]

    def element(put, s, at, points, total):
        x = [put[32 * s + 8 * k : 32 * s + 8 * k + 8, :] for k in range(3)]
        weight = put[32 * s + 24 : 32 * s + 32, :]
        residual = [
            points[k] - (at[12] * (at[3 * k] * x[0] + at[3 * k + 1] * x[1] + at[3 * k + 2] * x[2]) + at[9 + k])
            for k in range(3)
        ]
        squared = SOFTEN + residual[0] * residual[0] + residual[1] * residual[1] + residual[2] * residual[2]
        pull = weight * lax.rsqrt(squared)
        grads = [pull * residual[k] for k in range(3)]
        sized = [at[12] * grads[k] for k in range(3)]
        terms = [sized[k] * x[n] for k in range(3) for n in range(3)] + grads
        total = terms if total is None else [a + b for a, b in zip(total, terms)]
        return grads, total

    def moments(grads, value, u, v, total):
        h = [grads[k] * value for k in range(3)]
        terms = [h[k] * u for k in range(3)] + [h[k] * v for k in range(3)] + h + list(grads)
        return terms if total is None else [a + b for a, b in zip(total, terms)]

    def rays(at, t, down, value):
        u = uv[t, 0]
        v = uv[t, 1] + down
        across = at(13 + t) * value
        below = v / at(12) * value
        z3 = [at(k) * across + at(3 + k) * below + at(6 + k) * value for k in range(3)]
        return u, v, z3, [z3[k] + at(9 + k) for k in range(3)]

    def pair_at(jj):
        rows = slice(8 * jj, 8 * jj + 8)
        return [turn[k, rows, :] for k in range(13)]

    def camera_grad(values, total):
        turned, unit, length = rotation(values[0:4])
        focal = exact_exp(values[7])
        h = [[Pair.of(total[k]) / focal, Pair.of(total[3 + k]) / focal, Pair.of(total[6 + k])] for k in range(3)]
        along = turned[0][0] * h[0][0] + turned[0][1] * h[0][1]
        for k in range(1, 3):
            along = along + turned[k][0] * h[k][0] + turned[k][1] * h[k][1]
        return rotation_grad(h, unit, length) + [total[9], total[10], total[11], -along.high]

    def add_slots(ref, count):
        total = ref[0]
        for p in range(1, count):
            total = total + ref[p]
        return total

    def step(st, carry):
        late = (st > 0).astype(F32)
        fix_one = (1.0 - BETA_ONE) + late * ((1.0 - BETA_ONE**2) - (1.0 - BETA_ONE))
        fix_two = (1.0 - BETA_TWO) + late * ((1.0 - BETA_TWO**2) - (1.0 - BETA_TWO))

        now = depth[...]
        for x in range(2):
            all_depth[st, r, x] = now[4 * x : 4 * x + 4, :]
        to_column(lambda row: pltpu.make_async_remote_copy(
            src_ref=all_depth.at[st, r], dst_ref=all_depth.at[st, r], send_sem=send_sem.at[OWN_DEPTH],
            recv_sem=all_sem.at[st, r], device_id=(row, c), device_id_type=MESH).start())
        row_depth[st, g] = now
        to_row_group(lambda p, row, col: remote(
            row_depth.at[st, g], row_depth.at[st, g], ROW_DEPTH, st, (row, col)).start())

        def pass_on(row):
            for x in range(2):
                p = 2 * row + x

                @pl.when(p != g)
                def _():
                    remote(all_depth.at[st, row, x], col_depth.at[st, g], COL_DEPTH, st, (r, 2 * p + q)).start()

        pass_on(r)

        @pl.when(st == 0)
        def _():
            remote(first_pose.at[q], first_pose.at[q], FIRST_POSE, 0, sibling).start()
            repeat(CHIPS // 2, swap_strip)

        sums[st, q] = jnp.zeros((12, 32, LANES), F32)
        acc_row[...] = jnp.zeros_like(acc_row)
        acc_col[...] = jnp.zeros_like(acc_col)

        def arrive(n, carry):
            row = row_near(n)
            wait_bytes(all_depth.at[st, row], all_sem.at[st, row])
            pass_on(row)
            return carry

        lax.fori_loop(1, ROWS, arrive, 0)
        col_depth[st, g] = all_depth[st, z, x_lo]

        @pl.when(st == 0)
        def _():
            def rest(n):
                prepare(CHIPS // 2 + n)
                swap_strip(CHIPS // 2 + n)
            repeat(CHIPS // 2, rest)
            wait_bytes(first_pose.at[1 - q], recv_sem.at[FIRST_POSE, 0])
            for k in range(8):
                pose[k, 0:16, :] = first_pose[0, k]
                pose[k, 16:32, :] = first_pose[1, k]

        @pl.when(st > 0)
        def _():
            wait_bytes(cam_all.at[st - 1, pl.ds(0, 2 * ROWS - 1)], recv_sem.at[CAM_ALL, st - 1])
            cam[...], cam_m[...], cam_v[...] = adam_step(
                cam[...], add_slots(cam_all.at[st - 1], 2 * ROWS), cam_m[...], cam_v[...],
                1.0 - BETA_ONE, 1.0 - BETA_TWO, rates[1])

        values = cameras()
        turned = plain_rotation(*values[0:4])
        focal = jnp.exp(values[7])

        def keep_ray(ref, at, rows):
            for k in range(3):
                for n in range(3):
                    ref[at + (3 * n + k,)] = jnp.broadcast_to(turned[k][n][rows], (8, LANES))
                ref[at + (9 + k,)] = jnp.broadcast_to(values[4 + k][rows], (8, LANES))
            ref[at + (12,)] = jnp.broadcast_to(focal[rows], (8, LANES))
            for t in range(TILES):
                ref[at + (13 + t,)] = uv[t, 0] / ref[at + (12,)]

        keep_ray(row_ray, (), slice(0, 8))
        for jj in range(SECONDS):
            keep_ray(col_ray, (jj,), slice(8 + jj, 9 + jj))
        values = [pose[k] for k in range(8)]
        turned = plain_rotation(*values[0:4])
        for k in range(3):
            for n in range(3):
                turn[3 * k + n] = turned[k][n]
            turn[9 + k] = values[4 + k]
        turn[12] = jnp.exp(values[7])

        @pl.when(st == 0)
        def _():
            wait_bytes(planes.at[1 - q], recv_sem.at[SWAP, 0])

        wait_bytes(row_depth.at[st, pl.ds(0, CHIPS - 1)], recv_sem.at[ROW_DEPTH, st])

        def side_rows(n):
            m = chip_at(n)
            down = (4 * m).astype(F32)
            for t in range(TILES):
                value = jnp.exp(row_depth[st, m, :, t * LANES : (t + 1) * LANES])
                _, _, z3, points = rays(lambda k: row_ray[k], t, down, value)
                tmp[t, 6] = value
                for k in range(3):
                    tmp[t, k] = z3[k]
                    tmp[t, 7 + k] = points[k]
            for jj in range(SECONDS):
                at = pair_at(jj)
                total = None
                for t in range(TILES):
                    points = [tmp[t, 7 + k] for k in range(3)]
                    grads, total = element(planes.at[jj // 2, m, jj % 2, t], 0, at, points, total)
                    for k in range(3):
                        tmp[t, 3 + k] = grads[k] if jj == 0 else tmp[t, 3 + k] + grads[k]
                for k in range(12):
                    sums[st, q, k, 8 * jj : 8 * jj + 8, :] += total[k]
            total = None
            for t in range(TILES):
                grads = [tmp[t, 3 + k] for k in range(3)]
                z3 = [tmp[t, k] for k in range(3)]
                row_grad[m, :, t * LANES : (t + 1) * LANES] = (
                    grads[0] * z3[0] + grads[1] * z3[1] + grads[2] * z3[2])
                total = moments(grads, tmp[t, 6], uv[t, 0], uv[t, 1] + down, total)
            for k in range(12):
                acc_row[k] += total[k]

            @pl.when(n < CHIPS - 1)
            def _():
                remote(row_grad.at[m], row_recv.at[st, g], ROW_GRAD, st, (r, 2 * m + q)).start()

        repeat(CHIPS, side_rows)
        row_recv[st, g] = row_grad[g]
        wait_bytes(col_depth.at[st, pl.ds(0, CHIPS - 1)], recv_sem.at[COL_DEPTH, st])

        def side_cols(n):
            m = chip_at(n)
            down = (4 * m).astype(F32)
            values = jnp.exp(col_depth[st, m])
            for jj in range(SECONDS):
                at = pair_at(jj)
                total = None
                cam_total = None
                for t in range(TILES):
                    value = jnp.broadcast_to(values[jj : jj + 1, t * LANES : (t + 1) * LANES], (8, LANES))
                    u, v, z3, points = rays(lambda k: col_ray[jj, k], t, down, value)
                    grads, total = element(planes.at[jj // 2, m, jj % 2, t], 1, at, points, total)
                    mine = grads[0] * z3[0] + grads[1] * z3[1] + grads[2] * z3[2]
                    col_grad[m, jj : jj + 1, t * LANES : (t + 1) * LANES] = jnp.sum(mine, axis=0, keepdims=True)
                    cam_total = moments(grads, value, u, v, cam_total)
                for k in range(12):
                    sums[st, q, k, 8 * jj : 8 * jj + 8, :] += total[k]
                for k in range(12):
                    acc_col[k, jj] += cam_total[k]

            @pl.when(jnp.logical_not(inside & (m == g)))
            def _():
                remote(col_grad.at[m], col_recv.at[st, 2 * r + x_lo], COL_GRAD, st, (z, 2 * m + q)).start()

        repeat(CHIPS, side_cols)

        @pl.when(inside)
        def _():
            col_recv[st, 2 * r + x_lo] = col_grad[g]

        total = []
        for k in range(12):
            rows = [acc_row[k]] + [jnp.sum(acc_col[k, jj], axis=0, keepdims=True) for jj in range(SECONDS)]
            total.append(lane_sum(jnp.concatenate(rows + [jnp.zeros((4, LANES), F32)], axis=0)))
        part = camera_grad(cameras(), total)
        counted = (lane16 == image16) & (sub16 < 8 + SECONDS)
        cam_row[st, g] = jnp.concatenate(
            [jnp.sum(jnp.where(counted, part[k], 0.0), axis=0, keepdims=True) for k in range(8)], axis=0)
        to_row_group(lambda p, row, col: remote(
            cam_row.at[st, g], cam_row.at[st, g], CAM_ROW, st, (row, col)).start())
        remote(sums.at[st, q], sums.at[st, q], POSE, st, sibling).start()

        wait_bytes(all_depth.at[st, pl.ds(0, ROWS - 1)], send_sem.at[OWN_DEPTH])
        wait_bytes(col_depth.at[st, pl.ds(0, CHIPS - 1)], send_sem.at[COL_DEPTH])
        wait_bytes(row_depth.at[st, pl.ds(0, CHIPS - 1)], send_sem.at[ROW_DEPTH])

        wait_bytes(sums.at[st, 1 - q], recv_sem.at[POSE, st])
        values = [pose[k] for k in range(8)]
        total = [-lane_sum(sums[st, 0, k] + sums[st, 1, k]) for k in range(12)]
        turned, pull_back = jax.vjp(plain_rotation, *values[0:4])
        h = [[total[3 * k + n] for n in range(3)] for k in range(3)]
        grad_scale = sum(turned[k][n] * h[k][n] for k in range(3) for n in range(3))
        grads = list(pull_back(h)) + total[9:12] + [grad_scale]
        for k in range(8):
            pose[k], pose_m[k], pose_v[k] = adam_step(
                values[k], grads[k], pose_m[k], pose_v[k], fix_one, fix_two, rates[2])

        wait_bytes(cam_row.at[st, pl.ds(0, CHIPS - 1)], recv_sem.at[CAM_ROW, st])
        cam_all[st, 2 * r + q] = add_slots(cam_row.at[st], CHIPS)
        to_column_chips(lambda row, col: remote(
            cam_all.at[st, 2 * r + q], cam_all.at[st, 2 * r + q], CAM_ALL, st, (row, col)).start())

        wait_bytes(sums.at[st, q], send_sem.at[POSE])
        wait_bytes(row_recv.at[st, pl.ds(0, CHIPS - 1)], recv_sem.at[ROW_GRAD, st])
        grad = add_slots(row_recv.at[st], CHIPS)
        wait_bytes(row_recv.at[st, pl.ds(0, CHIPS - 1)], send_sem.at[ROW_GRAD])
        wait_bytes(cam_row.at[st, pl.ds(0, CHIPS - 1)], send_sem.at[CAM_ROW])
        wait_slots(col_recv.at[st], recv_sem.at[COL_GRAD, st])
        pieces = []
        for x in range(2):
            piece = col_recv[st, x]
            for p in range(1, ROWS):
                piece = piece + col_recv[st, 2 * p + x]
            pieces.append(piece)
        grad = grad + jnp.concatenate(pieces, axis=0)
        depth[...], depth_m[...], depth_v[...] = adam_step(
            depth[...], grad, depth_m[...], depth_v[...], fix_one, fix_two, rates[0])
        wait_slots(col_recv.at[st], send_sem.at[COL_GRAD])
        wait_bytes(cam_all.at[st, pl.ds(0, 2 * ROWS - 1)], send_sem.at[CAM_ALL])
        return carry

    lax.fori_loop(0, ADAM_STEPS, step, 0)

    last = ADAM_STEPS - 1
    wait_bytes(outbox, send_sem.at[SWAP])
    wait_bytes(first_pose.at[q], send_sem.at[FIRST_POSE])
    depth_out[...] = pltpu.roll(depth[...], (WIDE - 64 * q) % WIDE, 1)[:, 0:HALF]
    small = lax.broadcasted_iota(jnp.int32, (8, 8), 1)
    for j in range(2):
        packed = jnp.zeros((8, 8), F32)
        for k in range(8):
            mine = pose[k, pl.ds(pl.multiple_of(16 * q + 8 * j, 8), 8), :]
            packed = jnp.where(small == k, mine[:, 0:8], packed)
        pair_out[:, j, :] = packed
    wait_bytes(cam_all.at[last, pl.ds(0, 2 * ROWS - 1)], recv_sem.at[CAM_ALL, last])
    final, _, _ = adam_step(
        cam[...], add_slots(cam_all.at[last], 2 * ROWS), cam_m[...], cam_v[...],
        1.0 - BETA_ONE**2, 1.0 - BETA_TWO**2, rates[1])
    camera_out[...] = final[:, 0:IMAGES]


def body(pointmaps, confidence, valid_blocks, log_depth, camera, pair_pose, step_sizes):
    vmem = pl.BlockSpec(memory_space=pltpu.VMEM)
    hbm = pl.BlockSpec(memory_space=pl.ANY)
    steps = ADAM_STEPS
    maps = pointmaps.transpose(0, 1, 3, 2, 4)

    def f32(*shape):
        return pltpu.VMEM(shape, F32)

    depth, cam, pair = pl.pallas_call(
        kernel,
        out_shape=(
            jax.ShapeDtypeStruct(log_depth.shape, F32),
            jax.ShapeDtypeStruct((8, IMAGES), F32),
            jax.ShapeDtypeStruct(pair_pose.shape, F32),
        ),
        in_specs=[hbm, hbm, vmem, vmem, vmem, vmem, pl.BlockSpec(memory_space=pltpu.SMEM)],
        out_specs=(vmem, vmem, vmem),
        scratch_shapes=[
            pltpu.VMEM(maps.shape, jnp.bfloat16),
            pltpu.VMEM(confidence.shape, jnp.bfloat16),
            f32(2, CHIPS, 2, TILES, 64, LANES),
            f32(CHIPS, 2, TILES, 64, LANES),
            f32(TILES, 2, 8, LANES),
            f32(17, 8, LANES),
            f32(SECONDS, 17, 8, LANES),
            f32(13, 32, LANES),
            f32(TILES, 10, 8, LANES),
            f32(12, 8, LANES),
            f32(12, SECONDS, 8, LANES),
            f32(steps, 2, 12, 32, LANES),
            f32(8, WIDE), f32(8, WIDE), f32(8, WIDE),
            f32(2, 8, 16, LANES),
            f32(8, 32, LANES), f32(8, 32, LANES), f32(8, 32, LANES),
            f32(8, LANES), f32(8, LANES), f32(8, LANES),
            f32(steps, CHIPS, 8, WIDE),
            f32(steps, ROWS, 2, 4, WIDE),
            f32(steps, CHIPS, 4, WIDE),
            f32(CHIPS, 8, WIDE),
            f32(steps, CHIPS, 8, WIDE),
            f32(CHIPS, 4, WIDE),
            f32(steps, CHIPS, 4, WIDE),
            f32(steps, CHIPS, 8, LANES),
            f32(steps, 2 * ROWS, 8, LANES),
            pltpu.SemaphoreType.DMA((2,)),
            pltpu.SemaphoreType.DMA((KINDS,)),
            pltpu.SemaphoreType.DMA((KINDS, steps)),
            pltpu.SemaphoreType.DMA((steps, ROWS)),
        ],
        compiler_params=pltpu.CompilerParams(
            collective_id=0, has_side_effects=True, vmem_limit_bytes=56 * 1024 * 1024
        ),
        name="align",
    )(maps, confidence, valid_blocks, log_depth, camera.T, pair_pose, step_sizes)
    return depth, cam.T, pair


def solution(mesh):
    in_specs = (
        P("row", "col", None, None, None),
        P("row", "col", None, None),
        P("row", "col", None),
        P("row", "col"),
        P(),
        P("row", "col", None),
        P(),
    )
    out_specs = (P("row", "col"), P(), P("row", "col", None))
    return jax.shard_map(body, mesh=mesh, in_specs=in_specs, out_specs=out_specs, check_vma=False)
```

```python
import math

import jax
import jax.numpy as jnp
import numpy as np
from jax import lax
from jax.experimental import pallas as pl
from jax.experimental.pallas import tpu as pltpu
from jax.sharding import PartitionSpec as P

IMAGES = 64
IMG_WIDTH = 224
IMG_HEIGHT = 224
WIN_ROWS = 64
ADAM_STEPS = 2
BETA_ONE = 0.9
BETA_TWO = 0.999
ADAM_EPS = 0.001
SOFTEN = 0.01

ROWS = 8
COLS = 32
CHIPS = COLS // 2
SECONDS = 4
HALF = 448
WIDE = 512
TILES = 4
STRIP = 896
LANES = 128
MESH = pl.DeviceIdType.MESH
F32 = jnp.float32


def plain_rotation(w, x, y, z):
    length = jnp.sqrt(w * w + x * x + y * y + z * z)
    w, x, y, z = w / length, x / length, y / length, z / length
    return [
        [1.0 - 2.0 * (y * y + z * z), 2.0 * (x * y - w * z), 2.0 * (x * z + w * y)],
        [2.0 * (x * y + w * z), 1.0 - 2.0 * (x * x + z * z), 2.0 * (y * z - w * x)],
        [2.0 * (x * z - w * y), 2.0 * (y * z + w * x), 1.0 - 2.0 * (x * x + y * y)],
    ]


class Pair:
    def __init__(self, high, low):
        self.high = high
        self.low = low

    @staticmethod
    def of(value):
        return value if isinstance(value, Pair) else Pair(value, None)

    @staticmethod
    def closed(high, low):
        total = high + low
        return Pair(total, low - (total - high))

    @staticmethod
    def constant(value):
        high = float(np.float32(value))
        low = value - high
        return Pair(high, low if low else None)

    def __add__(self, other):
        other = Pair.of(other)
        total = self.high + other.high
        back = total - self.high
        rest = (self.high - (total - back)) + (other.high - back)
        for part in (self.low, other.low):
            rest = rest if part is None else rest + part
        return Pair.closed(total, rest)

    def __neg__(self):
        return Pair(-self.high, None if self.low is None else -self.low)

    def __sub__(self, other):
        return self + (-Pair.of(other))

    def twice(self):
        return Pair(2.0 * self.high, None if self.low is None else 2.0 * self.low)

    @staticmethod
    def split(value):
        wide = 4097.0 * value
        top = wide - (wide - value)
        return top, value - top

    def __mul__(self, other):
        other = Pair.of(other)
        product = self.high * other.high
        a, b = Pair.split(self.high)
        c, d = Pair.split(other.high)
        rest = ((a * c - product) + a * d + b * c) + b * d
        if self.low is not None:
            rest = rest + self.low * other.high
        if other.low is not None:
            rest = rest + self.high * other.low
        return Pair.closed(product, rest)

    def __truediv__(self, other):
        other = Pair.of(other)
        first = self.high / other.high
        rest = self - other * Pair(first, None)
        return Pair.closed(first, rest.high / other.high)

    def root(self):
        first = jnp.sqrt(self.high)
        rest = self - Pair(first, None) * Pair(first, None)
        return Pair.closed(first, rest.high / (2.0 * first))


def exact_exp(value):
    small = Pair(value * 0.0625, None)
    total = Pair.constant(1.0 / math.factorial(12))
    total = Pair(jnp.full_like(value, total.high), None)
    for k in range(11, -1, -1):
        total = total * small + Pair.constant(1.0 / math.factorial(k))
    for _ in range(4):
        total = total * total
    return total


def rotation(quaternion):
    w, x, y, z = [Pair.of(value) for value in quaternion]
    length = (w * w + x * x + y * y + z * z).root()
    w, x, y, z = w / length, x / length, y / length, z / length
    xx, yy, zz = x * x, y * y, z * z
    xy, xz, yz, wx, wy, wz = x * y, x * z, y * z, w * x, w * y, w * z
    one = Pair(1.0, None)
    turned = [
        [one - (yy + zz).twice(), (xy - wz).twice(), (xz + wy).twice()],
        [(xy + wz).twice(), one - (xx + zz).twice(), (yz - wx).twice()],
        [(xz - wy).twice(), (yz + wx).twice(), one - (xx + yy).twice()],
    ]
    return turned, (w, x, y, z), length


def rotation_grad(h, unit, length):
    w, x, y, z = unit
    sums = [h[0][1] + h[1][0], h[0][2] + h[2][0], h[1][2] + h[2][1]]
    turns = [h[2][1] - h[1][2], h[0][2] - h[2][0], h[1][0] - h[0][1]]
    dw = (z * turns[2] + y * turns[1] + x * turns[0]).twice()
    dx = (y * sums[0] + z * sums[1] + w * turns[0] - (x * (h[1][1] + h[2][2])).twice()).twice()
    dy = (x * sums[0] + z * sums[2] + w * turns[1] - (y * (h[0][0] + h[2][2])).twice()).twice()
    dz = (x * sums[1] + y * sums[2] + w * turns[2] - (z * (h[0][0] + h[1][1])).twice()).twice()
    along = w * dw + x * dx + y * dy + z * dz
    return [((part - axis * along) / length).high for part, axis in ((dw, w), (dx, x), (dy, y), (dz, z))]


def adam_step(param, grad, first, second, fix_one, fix_two, step_size):
    first = BETA_ONE * first + (1.0 - BETA_ONE) * grad
    second = BETA_TWO * second + (1.0 - BETA_TWO) * grad * grad
    update = step_size * (first / fix_one) / (jnp.sqrt(second / fix_two) + ADAM_EPS)
    return param - update, first, second


def lane_sum(value):
    return jnp.broadcast_to(jnp.sum(value, axis=1, keepdims=True), value.shape)


COL_DEPTH, ROW_DEPTH, ROW_GRAD, COL_GRAD, POSE, CAM_ROW, CAM_ALL, SWAP, FIRST_POSE, OWN_DEPTH = range(10)
KINDS = 10


def kernel(
    maps_hbm, conf_hbm, valid_ref, depth_in, camera_in, pair_in, rates,
    packed_out,
    raw, raw_conf, planes, outbox, uv, row_ray, col_ray, turn, tmp, acc_row, acc_col, sums,
    depth, depth_m, depth_v, first_pose, pose, pose_m, pose_v, cam, cam_m, cam_v,
    row_depth, all_depth, col_depth, row_grad, row_recv, col_grad, col_recv, cam_row, cam_all,
    load_sem, send_sem, recv_sem, all_sem,
):
    r = lax.axis_index("row")
    c = lax.axis_index("col")
    q = lax.rem(c, 2)
    g = lax.div(c, 2)
    z = lax.div(g, 2)
    x_lo = lax.rem(g, 2)
    inside = r == z
    sibling = (r, 2 * g + 1 - q)
    lane = lax.broadcasted_iota(jnp.int32, (8, LANES), 1)
    sub = lax.broadcasted_iota(jnp.int32, (8, LANES), 0)

    def chip_at(n):
        half = lax.div(n + 1, 2)
        return lax.rem(g + 8 + half * (1 - 2 * lax.rem(n, 2)), CHIPS)

    def remote(src, dst, kind, st, device):
        return pltpu.make_async_remote_copy(
            src_ref=src, dst_ref=dst, send_sem=send_sem.at[kind], recv_sem=recv_sem.at[kind, st],
            device_id=device, device_id_type=MESH,
        )

    def wait_bytes(ref, sem):
        pltpu.make_async_copy(ref, ref, sem).wait()

    def wait_slots(ref, sem):
        @pl.when(inside)
        def _():
            wait_bytes(ref.at[pl.ds(0, CHIPS - 1)], sem)

        @pl.when(jnp.logical_not(inside))
        def _():
            wait_bytes(ref, sem)

    def repeat(count, action):
        def one(n, carry):
            action(n)
            return carry
        lax.fori_loop(0, count, one, 0)

    load_maps = pltpu.make_async_copy(maps_hbm, raw, load_sem.at[0])
    load_conf = pltpu.make_async_copy(conf_hbm, raw_conf, load_sem.at[1])
    load_maps.start()
    load_conf.start()

    barrier = pltpu.get_barrier_semaphore()

    def greet(row, col):
        pl.semaphore_signal(barrier, inc=1, device_id=(row, col), device_id_type=MESH)

    def to_row_group(act):
        def one(n):
            p = chip_at(n)
            act(p, r, 2 * p + q)
        repeat(CHIPS - 1, one)

    def row_near(n):
        across = lax.div(n, 4)
        turn_y = lax.rem(n, 4)
        turn_y = turn_y + lax.div(turn_y, 2) - 2 * lax.div(turn_y, 3)
        return 4 * lax.rem(lax.div(r, 4) + across, 2) + lax.rem(lax.rem(r, 4) + turn_y, 4)

    def to_column(act):
        lax.fori_loop(1, ROWS, lambda n, carry: (act(row_near(ROWS - n)), carry)[1], 0)

    def to_column_chips(act):
        def one(n):
            act(lax.rem(r + lax.div(n, 2), ROWS), 2 * g + lax.rem(q + lax.rem(n, 2), 2))
        lax.fori_loop(1, 2 * ROWS, lambda n, carry: (one(n), carry)[1], 0)

    to_row_group(lambda p, row, col: greet(row, col))
    to_column(lambda row: greet(row, c))
    greet(*sibling)

    depth[...] = jnp.zeros_like(depth)
    depth[:, 0:HALF] = depth_in[...]
    depth[...] = pltpu.roll(depth[...], 64 * q, 1)
    for ref in (depth_m, depth_v, pose_m, pose_v, cam, cam_m, cam_v):
        ref[...] = jnp.zeros_like(ref)
    for j in range(2):
        loaded = pair_in[:, j, :]
        for k in range(8):
            first_pose[q, k, 8 * j : 8 * j + 8, :] = jnp.broadcast_to(loaded[:, k : k + 1], (8, LANES))
    cam[:, 0:IMAGES] = camera_in[...]
    for t in range(TILES):
        position = lane + (3 * q + t) * LANES
        downward = (
            (position >= IMG_WIDTH).astype(jnp.int32)
            + (position >= 2 * IMG_WIDTH).astype(jnp.int32)
            + (position >= 3 * IMG_WIDTH).astype(jnp.int32)
        )
        uv[t, 0] = (position - IMG_WIDTH * downward).astype(F32) - (IMG_WIDTH - 1) / 2.0
        uv[t, 1] = downward.astype(F32) + ((IMG_HEIGHT - WIN_ROWS) // 2 - (IMG_HEIGHT - 1) / 2.0)

    def prepare(m):
        lane64 = lax.broadcasted_iota(jnp.int32, (8, WIN_ROWS), 1)
        for away in (True, False):
            half = 1 - q if away else q
            for j in range(2):
                here = valid_ref[:, j, :].astype(F32)
                other = (ROWS * r + sub) != (2 * c + j)
                scale = jnp.where(other, 1.0 / (2.0 * (IMAGES - 1)), 0.0)
                line = [
                    scale * lane_sum_to(jnp.where(lane64 == 4 * m + 2 * half + a, here, 0.0)) for a in range(2)
                ]
                for t in range(TILES):
                    tile = 3 * half + t
                    start = pl.multiple_of(m * STRIP + tile * LANES, LANES)
                    put = outbox.at[m, j, t] if away else planes.at[q, m, j, t]
                    for i in range(8):
                        for k in range(3):
                            put[pl.ds(8 * k + i, 2, stride=32), :] = raw[i, j, k, :, pl.ds(start, LANES)].astype(F32)
                        put[pl.ds(24 + i, 2, stride=32), :] = raw_conf[i, j, :, pl.ds(start, LANES)].astype(F32)
                    position = lane + tile * LANES - HALF * half
                    keep = jnp.where(position < IMG_WIDTH, line[0], line[1])
                    keep = jnp.where((position >= 0) & (position < HALF), keep, 0.0)
                    for s in range(2):
                        put[32 * s + 24 : 32 * s + 32, :] = put[32 * s + 24 : 32 * s + 32, :] * keep

    def lane_sum_to(value):
        return jnp.broadcast_to(jnp.sum(value, axis=1, keepdims=True), (8, LANES))

    def swap_strip(m):
        remote(outbox.at[m], planes.at[q, m], SWAP, 0, sibling).start()

    load_maps.wait()
    load_conf.wait()
    repeat(CHIPS // 2, prepare)
    pl.semaphore_wait(barrier, CHIPS - 1 + ROWS - 1 + 1)

    lane16 = lax.broadcasted_iota(jnp.int32, (16, LANES), 1)
    sub16 = lax.broadcasted_iota(jnp.int32, (16, LANES), 0)
    image16 = jnp.where(sub16 < 8, 8 * r + sub16, SECONDS * g + lax.rem(sub16, SECONDS))

    def cameras():
        now = cam[...]
        return [
            lane_sum(jnp.where(lane16 == image16, jnp.broadcast_to(now[k : k + 1, :], (16, LANES)), 0.0))
            for k in range(8)
        ]

    def element(put, s, at, points, total):
        x = [put[32 * s + 8 * k : 32 * s + 8 * k + 8, :] for k in range(3)]
        weight = put[32 * s + 24 : 32 * s + 32, :]
        residual = [
            points[k] - (at[12] * (at[3 * k] * x[0] + at[3 * k + 1] * x[1] + at[3 * k + 2] * x[2]) + at[9 + k])
            for k in range(3)
        ]
        squared = SOFTEN + residual[0] * residual[0] + residual[1] * residual[1] + residual[2] * residual[2]
        pull = weight * lax.rsqrt(squared)
        grads = [pull * residual[k] for k in range(3)]
        sized = [at[12] * grads[k] for k in range(3)]
        terms = [sized[k] * x[n] for k in range(3) for n in range(3)] + grads
        total = terms if total is None else [a + b for a, b in zip(total, terms)]
        return grads, total

    def moments(grads, value, u, v, total):
        h = [grads[k] * value for k in range(3)]
        terms = [h[k] * u for k in range(3)] + [h[k] * v for k in range(3)] + h + list(grads)
        return terms if total is None else [a + b for a, b in zip(total, terms)]

    def rays(at, t, down, value):
        u = uv[t, 0]
        v = uv[t, 1] + down
        across = at(13 + t) * value
        below = v / at(12) * value
        z3 = [at(k) * across + at(3 + k) * below + at(6 + k) * value for k in range(3)]
        return u, v, z3, [z3[k] + at(9 + k) for k in range(3)]

    def pair_at(jj):
        rows = slice(8 * jj, 8 * jj + 8)
        return [turn[k, rows, :] for k in range(13)]

    def camera_grad(values, total):
        turned, unit, length = rotation(values[0:4])
        focal = exact_exp(values[7])
        h = [[Pair.of(total[k]) / focal, Pair.of(total[3 + k]) / focal, Pair.of(total[6 + k])] for k in range(3)]
        along = turned[0][0] * h[0][0] + turned[0][1] * h[0][1]
        for k in range(1, 3):
            along = along + turned[k][0] * h[k][0] + turned[k][1] * h[k][1]
        return rotation_grad(h, unit, length) + [total[9], total[10], total[11], -along.high]

    def add_slots(ref, count):
        total = ref[0]
        for p in range(1, count):
            total = total + ref[p]
        return total

    def step(st, carry):
        late = (st > 0).astype(F32)
        fix_one = (1.0 - BETA_ONE) + late * ((1.0 - BETA_ONE**2) - (1.0 - BETA_ONE))
        fix_two = (1.0 - BETA_TWO) + late * ((1.0 - BETA_TWO**2) - (1.0 - BETA_TWO))

        now = depth[...]
        for x in range(2):
            all_depth[st, r, x] = now[4 * x : 4 * x + 4, :]
        to_column(lambda row: pltpu.make_async_remote_copy(
            src_ref=all_depth.at[st, r], dst_ref=all_depth.at[st, r], send_sem=send_sem.at[OWN_DEPTH],
            recv_sem=all_sem.at[st, r], device_id=(row, c), device_id_type=MESH).start())
        row_depth[st, g] = now
        to_row_group(lambda p, row, col: remote(
            row_depth.at[st, g], row_depth.at[st, g], ROW_DEPTH, st, (row, col)).start())

        def pass_on(row):
            for x in range(2):
                p = 2 * row + x

                @pl.when(p != g)
                def _():
                    remote(all_depth.at[st, row, x], col_depth.at[st, g], COL_DEPTH, st, (r, 2 * p + q)).start()

        pass_on(r)

        @pl.when(st == 0)
        def _():
            remote(first_pose.at[q], first_pose.at[q], FIRST_POSE, 0, sibling).start()
            repeat(CHIPS // 2, swap_strip)

        sums[st, q] = jnp.zeros((12, 32, LANES), F32)
        acc_row[...] = jnp.zeros_like(acc_row)
        acc_col[...] = jnp.zeros_like(acc_col)

        def arrive(n, carry):
            row = row_near(n)
            wait_bytes(all_depth.at[st, row], all_sem.at[st, row])
            pass_on(row)
            return carry

        lax.fori_loop(1, ROWS, arrive, 0)
        col_depth[st, g] = all_depth[st, z, x_lo]

        @pl.when(st == 0)
        def _():
            def rest(n):
                prepare(CHIPS // 2 + n)
                swap_strip(CHIPS // 2 + n)
            repeat(CHIPS // 2, rest)
            wait_bytes(first_pose.at[1 - q], recv_sem.at[FIRST_POSE, 0])
            for k in range(8):
                pose[k, 0:16, :] = first_pose[0, k]
                pose[k, 16:32, :] = first_pose[1, k]

        @pl.when(st > 0)
        def _():
            wait_bytes(cam_all.at[st - 1, pl.ds(0, 2 * ROWS - 1)], recv_sem.at[CAM_ALL, st - 1])
            cam[...], cam_m[...], cam_v[...] = adam_step(
                cam[...], add_slots(cam_all.at[st - 1], 2 * ROWS), cam_m[...], cam_v[...],
                1.0 - BETA_ONE, 1.0 - BETA_TWO, rates[1])

        values = cameras()
        turned = plain_rotation(*values[0:4])
        focal = jnp.exp(values[7])

        def keep_ray(ref, at, rows):
            for k in range(3):
                for n in range(3):
                    ref[at + (3 * n + k,)] = jnp.broadcast_to(turned[k][n][rows], (8, LANES))
                ref[at + (9 + k,)] = jnp.broadcast_to(values[4 + k][rows], (8, LANES))
            ref[at + (12,)] = jnp.broadcast_to(focal[rows], (8, LANES))
            for t in range(TILES):
                ref[at + (13 + t,)] = uv[t, 0] / ref[at + (12,)]

        keep_ray(row_ray, (), slice(0, 8))
        for jj in range(SECONDS):
            keep_ray(col_ray, (jj,), slice(8 + jj, 9 + jj))
        values = [pose[k] for k in range(8)]
        turned = plain_rotation(*values[0:4])
        for k in range(3):
            for n in range(3):
                turn[3 * k + n] = turned[k][n]
            turn[9 + k] = values[4 + k]
        turn[12] = jnp.exp(values[7])

        @pl.when(st == 0)
        def _():
            wait_bytes(planes.at[1 - q], recv_sem.at[SWAP, 0])

        wait_bytes(row_depth.at[st, pl.ds(0, CHIPS - 1)], recv_sem.at[ROW_DEPTH, st])

        def side_rows(n):
            m = chip_at(n)
            down = (4 * m).astype(F32)
            for t in range(TILES):
                value = jnp.exp(row_depth[st, m, :, t * LANES : (t + 1) * LANES])
                _, _, z3, points = rays(lambda k: row_ray[k], t, down, value)
                tmp[t, 6] = value
                for k in range(3):
                    tmp[t, k] = z3[k]
                    tmp[t, 7 + k] = points[k]
            for jj in range(SECONDS):
                at = pair_at(jj)
                total = None
                for t in range(TILES):
                    points = [tmp[t, 7 + k] for k in range(3)]
                    grads, total = element(planes.at[jj // 2, m, jj % 2, t], 0, at, points, total)
                    for k in range(3):
                        tmp[t, 3 + k] = grads[k] if jj == 0 else tmp[t, 3 + k] + grads[k]
                for k in range(12):
                    sums[st, q, k, 8 * jj : 8 * jj + 8, :] += total[k]
            total = None
            for t in range(TILES):
                grads = [tmp[t, 3 + k] for k in range(3)]
                z3 = [tmp[t, k] for k in range(3)]
                row_grad[m, :, t * LANES : (t + 1) * LANES] = (
                    grads[0] * z3[0] + grads[1] * z3[1] + grads[2] * z3[2])
                total = moments(grads, tmp[t, 6], uv[t, 0], uv[t, 1] + down, total)
            for k in range(12):
                acc_row[k] += total[k]

            @pl.when(n < CHIPS - 1)
            def _():
                remote(row_grad.at[m], row_recv.at[st, g], ROW_GRAD, st, (r, 2 * m + q)).start()

        repeat(CHIPS, side_rows)
        row_recv[st, g] = row_grad[g]
        wait_bytes(col_depth.at[st, pl.ds(0, CHIPS - 1)], recv_sem.at[COL_DEPTH, st])

        def side_cols(n):
            m = chip_at(n)
            down = (4 * m).astype(F32)
            values = jnp.exp(col_depth[st, m])
            for jj in range(SECONDS):
                at = pair_at(jj)
                total = None
                cam_total = None
                for t in range(TILES):
                    value = jnp.broadcast_to(values[jj : jj + 1, t * LANES : (t + 1) * LANES], (8, LANES))
                    u, v, z3, points = rays(lambda k: col_ray[jj, k], t, down, value)
                    grads, total = element(planes.at[jj // 2, m, jj % 2, t], 1, at, points, total)
                    mine = grads[0] * z3[0] + grads[1] * z3[1] + grads[2] * z3[2]
                    col_grad[m, jj : jj + 1, t * LANES : (t + 1) * LANES] = jnp.sum(mine, axis=0, keepdims=True)
                    cam_total = moments(grads, value, u, v, cam_total)
                for k in range(12):
                    sums[st, q, k, 8 * jj : 8 * jj + 8, :] += total[k]
                for k in range(12):
                    acc_col[k, jj] += cam_total[k]

            @pl.when(jnp.logical_not(inside & (m == g)))
            def _():
                remote(col_grad.at[m], col_recv.at[st, 2 * r + x_lo], COL_GRAD, st, (z, 2 * m + q)).start()

        repeat(CHIPS, side_cols)

        @pl.when(inside)
        def _():
            col_recv[st, 2 * r + x_lo] = col_grad[g]

        total = []
        for k in range(12):
            rows = [acc_row[k]] + [jnp.sum(acc_col[k, jj], axis=0, keepdims=True) for jj in range(SECONDS)]
            total.append(lane_sum(jnp.concatenate(rows + [jnp.zeros((4, LANES), F32)], axis=0)))
        part = camera_grad(cameras(), total)
        counted = (lane16 == image16) & (sub16 < 8 + SECONDS)
        cam_row[st, g] = jnp.concatenate(
            [jnp.sum(jnp.where(counted, part[k], 0.0), axis=0, keepdims=True) for k in range(8)], axis=0)
        to_row_group(lambda p, row, col: remote(
            cam_row.at[st, g], cam_row.at[st, g], CAM_ROW, st, (row, col)).start())
        remote(sums.at[st, q], sums.at[st, q], POSE, st, sibling).start()

        wait_bytes(all_depth.at[st, pl.ds(0, ROWS - 1)], send_sem.at[OWN_DEPTH])
        wait_bytes(col_depth.at[st, pl.ds(0, CHIPS - 1)], send_sem.at[COL_DEPTH])
        wait_bytes(row_depth.at[st, pl.ds(0, CHIPS - 1)], send_sem.at[ROW_DEPTH])

        wait_bytes(sums.at[st, 1 - q], recv_sem.at[POSE, st])
        values = [pose[k] for k in range(8)]
        total = [-lane_sum(sums[st, 0, k] + sums[st, 1, k]) for k in range(12)]
        turned, pull_back = jax.vjp(plain_rotation, *values[0:4])
        h = [[total[3 * k + n] for n in range(3)] for k in range(3)]
        grad_scale = sum(turned[k][n] * h[k][n] for k in range(3) for n in range(3))
        grads = list(pull_back(h)) + total[9:12] + [grad_scale]
        for k in range(8):
            pose[k], pose_m[k], pose_v[k] = adam_step(
                values[k], grads[k], pose_m[k], pose_v[k], fix_one, fix_two, rates[2])

        wait_bytes(cam_row.at[st, pl.ds(0, CHIPS - 1)], recv_sem.at[CAM_ROW, st])
        cam_all[st, 2 * r + q] = add_slots(cam_row.at[st], CHIPS)
        to_column_chips(lambda row, col: remote(
            cam_all.at[st, 2 * r + q], cam_all.at[st, 2 * r + q], CAM_ALL, st, (row, col)).start())

        wait_bytes(sums.at[st, q], send_sem.at[POSE])
        wait_bytes(row_recv.at[st, pl.ds(0, CHIPS - 1)], recv_sem.at[ROW_GRAD, st])
        grad = add_slots(row_recv.at[st], CHIPS)
        wait_bytes(row_recv.at[st, pl.ds(0, CHIPS - 1)], send_sem.at[ROW_GRAD])
        wait_bytes(cam_row.at[st, pl.ds(0, CHIPS - 1)], send_sem.at[CAM_ROW])
        wait_slots(col_recv.at[st], recv_sem.at[COL_GRAD, st])
        pieces = []
        for x in range(2):
            piece = col_recv[st, x]
            for p in range(1, ROWS):
                piece = piece + col_recv[st, 2 * p + x]
            pieces.append(piece)
        grad = grad + jnp.concatenate(pieces, axis=0)
        depth[...], depth_m[...], depth_v[...] = adam_step(
            depth[...], grad, depth_m[...], depth_v[...], fix_one, fix_two, rates[0])
        wait_slots(col_recv.at[st], send_sem.at[COL_GRAD])
        wait_bytes(cam_all.at[st, pl.ds(0, 2 * ROWS - 1)], send_sem.at[CAM_ALL])
        return carry

    lax.fori_loop(0, ADAM_STEPS, step, 0)

    last = ADAM_STEPS - 1
    wait_bytes(outbox, send_sem.at[SWAP])
    wait_bytes(first_pose.at[q], send_sem.at[FIRST_POSE])
    packed_out[:, 0:WIDE] = pltpu.roll(depth[...], (WIDE - 64 * q) % WIDE, 1)
    poses = jnp.zeros((8, LANES), F32)
    for j in range(2):
        for k in range(8):
            mine = pose[k, pl.ds(pl.multiple_of(16 * q + 8 * j, 8), 8), :]
            poses = jnp.where(lane == 8 * j + k, mine, poses)
    packed_out[:, WIDE + LANES : WIDE + 2 * LANES] = poses
    wait_bytes(cam_all.at[last, pl.ds(0, 2 * ROWS - 1)], recv_sem.at[CAM_ALL, last])
    final, _, _ = adam_step(
        cam[...], add_slots(cam_all.at[last], 2 * ROWS), cam_m[...], cam_v[...],
        1.0 - BETA_ONE**2, 1.0 - BETA_TWO**2, rates[1])
    packed_out[:, WIDE : WIDE + LANES] = final


def unpack(packed, depth_out, camera_out, pair_out):
    depth_out[...] = packed[:, 0:HALF]
    camera_out[...] = packed[:, WIDE : WIDE + IMAGES]
    poses = packed[:, WIDE + LANES : WIDE + 2 * LANES]
    pair_out[:, 0, :] = poses[:, 0:8]
    pair_out[:, 1, :] = poses[:, 8:16]


def body(pointmaps, confidence, valid_blocks, log_depth, camera, pair_pose, step_sizes):
    vmem = pl.BlockSpec(memory_space=pltpu.VMEM)
    hbm = pl.BlockSpec(memory_space=pl.ANY)
    steps = ADAM_STEPS
    maps = pointmaps.transpose(0, 1, 3, 2, 4)

    def f32(*shape):
        return pltpu.VMEM(shape, F32)

    packed = pl.pallas_call(
        kernel,
        out_shape=jax.ShapeDtypeStruct((8, WIDE + 2 * LANES), F32),
        in_specs=[hbm, hbm, vmem, vmem, vmem, vmem, pl.BlockSpec(memory_space=pltpu.SMEM)],
        out_specs=vmem,
        scratch_shapes=[
            pltpu.VMEM(maps.shape, jnp.bfloat16),
            pltpu.VMEM(confidence.shape, jnp.bfloat16),
            f32(2, CHIPS, 2, TILES, 64, LANES),
            f32(CHIPS, 2, TILES, 64, LANES),
            f32(TILES, 2, 8, LANES),
            f32(17, 8, LANES),
            f32(SECONDS, 17, 8, LANES),
            f32(13, 32, LANES),
            f32(TILES, 10, 8, LANES),
            f32(12, 8, LANES),
            f32(12, SECONDS, 8, LANES),
            f32(steps, 2, 12, 32, LANES),
            f32(8, WIDE), f32(8, WIDE), f32(8, WIDE),
            f32(2, 8, 16, LANES),
            f32(8, 32, LANES), f32(8, 32, LANES), f32(8, 32, LANES),
            f32(8, LANES), f32(8, LANES), f32(8, LANES),
            f32(steps, CHIPS, 8, WIDE),
            f32(steps, ROWS, 2, 4, WIDE),
            f32(steps, CHIPS, 4, WIDE),
            f32(CHIPS, 8, WIDE),
            f32(steps, CHIPS, 8, WIDE),
            f32(CHIPS, 4, WIDE),
            f32(steps, CHIPS, 4, WIDE),
            f32(steps, CHIPS, 8, LANES),
            f32(steps, 2 * ROWS, 8, LANES),
            pltpu.SemaphoreType.DMA((2,)),
            pltpu.SemaphoreType.DMA((KINDS,)),
            pltpu.SemaphoreType.DMA((KINDS, steps)),
            pltpu.SemaphoreType.DMA((steps, ROWS)),
        ],
        compiler_params=pltpu.CompilerParams(
            collective_id=0, has_side_effects=True, vmem_limit_bytes=56 * 1024 * 1024
        ),
        name="align",
    )(maps, confidence, valid_blocks, log_depth, camera.T, pair_pose, step_sizes)
    depth, cam, pair = pl.pallas_call(
        unpack,
        out_shape=(
            jax.ShapeDtypeStruct(log_depth.shape, F32),
            jax.ShapeDtypeStruct((8, IMAGES), F32),
            jax.ShapeDtypeStruct(pair_pose.shape, F32),
        ),
        in_specs=[vmem],
        out_specs=(vmem, vmem, vmem),
        name="unpack",
    )(packed)
    return depth, cam.T, pair


def solution(mesh):
    in_specs = (
        P("row", "col", None, None, None),
        P("row", "col", None, None),
        P("row", "col", None),
        P("row", "col"),
        P(),
        P("row", "col", None),
        P(),
    )
    out_specs = (P("row", "col"), P(), P("row", "col", None))
    return jax.shard_map(body, mesh=mesh, in_specs=in_specs, out_specs=out_specs, check_vma=False)
```
